32 devices in a mesh: ens: 2 (over y), lon: 4 (over z), lat: 2 (over x), ch: 2 (over core).
Axes of the slice: x: 2, y: 2, z: 4, core: 2. Of those that a mesh axis runs over, the one named last changes fastest.
Arguments:
- inputs: bfloat16 [128, 4096, 768], P(('ens', 'lat'), 'lon', 'ch'), parts along dimension 0, may hold values from -6 to 6
- cotangent: bfloat16 [128, 4096, 768], P(('ens', 'lat'), 'lon', 'ch'), parts along dimension 0, may hold values from -12 to 12
- first_weight: bfloat16 [2, 4, 2, 96, 96], P('ch', 'lat'), may hold values from -0.4375 to 0.4375
- first_bias: float32 [2, 4, 2, 96], P('ch', 'lat'), may hold values from -3 to 3
- second_weight: bfloat16 [2, 4, 2, 96, 96], P('ch', 'lat'), may hold values from -0.4375 to 0.4375
- counts: int32 [2, 4], P('ch', 'lat'), may hold values from 16 to 32, as said below
- keep_flags: int32 [64, 32, 2, 4], P(None, 'lon', 'ch', 'lat'), may hold values 0 or 1
Outputs:
- input_grad: bfloat16 [128, 4096, 768], P(('ens', 'lat'), 'lon', 'ch'), parts along dimension 0
- first_grad: float32 [4, 4, 2, 96, 96], P(('ens', 'ch'), 'lat'), parts along dimension 0
- second_grad: float32 [4, 4, 2, 96, 96], P(('ens', 'ch'), 'lat'), parts along dimension 0
- first_bias_grad: float32 [4, 4, 2, 96], P(('ens', 'ch'), 'lat'), parts along dimension 0
- second_bias_grad: float32 [4, 4, 2, 96], P(('ens', 'ch'), 'lat'), parts along dimension 0
The draws below stay inside these ranges and needn't reach their ends.
There are 2 independent parts, one for each index of `ens`. The reference program is written for one: setup_inputs(seed, part) draws one part's arguments, and reference() takes and returns one part's arrays. A program takes and returns all parts, laid end to end along the dimension named above; an argument that names none is the same for every part. Nothing has to cross between parts.
Inputs may be any that keep to these rules, and one draw needn't show every extreme that they name: Block b keeps longitude modes below counts[b]; some block keeps all 32 and some keeps 32 / 2.
All inputs are finite; a program needn't handle non-finite values. No bound on the sum of `keep_flags` on one device may be relied on, other than what follows from the above.
Results may differ from the reference program's by a relative error of at most 0.001.
Values may be sent and summed in bfloat16 or wider, within the bound.
A program may use at most 192 MiB of HBM per device.

```python
import math
import jax
import jax.numpy as jnp
from jax import lax

H = 64
W = 4096
C = 768
NB = 8
KM = 32
BS = 96
N_CH = 2


def draw_counts(key, part):
    key = jax.random.fold_in(key, 11)
    key_values = jax.random.fold_in(key, 1)
    key_order = jax.random.fold_in(key, 2)
    values = jax.random.randint(key_values, (NB,), KM // 2, KM + 1)
    order = jax.random.permutation(key_order, NB)
    values = values.at[order[0]].set(KM).at[order[1]].set(KM // 2)
    return values.reshape(N_CH, NB // N_CH).astype(jnp.int32)


def with_ends(array, key, least, top_value):
    longest = array.shape.index(max(array.shape))
    spots = []
    for shift in (0, 1):
        where = [jax.random.randint(jax.random.fold_in(key, axis), (), 0, length) for axis, length in enumerate(array.shape)]
        where[longest] = (where[longest] + shift) % array.shape[longest]
        spots.append(tuple(where))
    return array.at[spots[0]].set(least).at[spots[1]].set(top_value)


def steps_of(own_key, extent, pieces, least, top_value):
    loudness = 1.0
    for position, blocks in pieces:
        draws = jax.random.uniform(jax.random.fold_in(jax.random.fold_in(own_key, 6), position), (blocks,), jnp.float32, least / len(pieces), top_value / len(pieces))
        loudness = loudness * jnp.repeat(jnp.exp(draws), extent[position] // blocks).reshape((-1,) + (1,) * (len(extent) - 1 - position))
    return loudness


def normal_values(stream_key, extent, width, most, cuts=(), held_as=jnp.bfloat16):
    loudness = steps_of(stream_key, extent, cuts, -0.22, 0.18) if cuts else 1.0
    drawn = jax.random.normal(stream_key, extent, jnp.float32) * width * loudness
    return jnp.minimum(jnp.maximum(drawn, -most), most).astype(held_as)


def setup_inputs(seed: int = 0, part: int = 0) -> dict:
    arg_keys = jax.random.split(jax.random.key(seed), 8)
    part_keys = jax.random.split(jax.random.fold_in(arg_keys[7], part), 8)
    inputs = normal_values(part_keys[0], (H, W, C), 1.0, 6.0, ((0, 2), (1, 4), (2, 2)))
    cotangent = normal_values(part_keys[1], (H, W, C), 2.0, 12.0, ((0, 2), (1, 4), (2, 2)))
    first_weight = normal_values(arg_keys[2], (N_CH, NB // N_CH, 2, BS, BS), (2 * BS) ** -0.5, 0.4375, ((0, 2), (1, 2)))
    first_bias = normal_values(arg_keys[3], (N_CH, NB // N_CH, 2, BS), 0.5, 3.0, ((0, 2), (1, 2)), jnp.float32)
    second_weight = normal_values(arg_keys[4], (N_CH, NB // N_CH, 2, BS, BS), (2 * BS) ** -0.5, 0.4375, ((0, 2), (1, 2)))
    counts = draw_counts(jax.random.fold_in(arg_keys[7], 71), part)
    keep_flags = with_ends((jax.random.randint(arg_keys[6], (H, KM, N_CH, NB // N_CH), 0, 4) < 3).astype(jnp.int32), jax.random.fold_in(arg_keys[6], 1), 0, 1)
    return dict(inputs=inputs, cotangent=cotangent, first_weight=first_weight, first_bias=first_bias, second_weight=second_weight, counts=counts, keep_flags=keep_flags)


exact_precision = lax.Precision.HIGHEST

def wave_tables(modes, cells, length):
    phase = (modes[:, None] * cells[None, :] % length).astype(jnp.float32)
    angle = phase * (2.0 * math.pi / length)
    scale = 1.0 / math.sqrt(length)
    return (jnp.cos(angle) * scale, jnp.sin(angle) * scale)

def activate(real_part, imag_part):
    return (jax.nn.gelu(real_part, approximate=True), jax.nn.gelu(imag_part, approximate=True))

def mixing_grads(spec_real, spec_imag, error_real, error_imag, weight_mask, first, bias, second):
    first_real = first[:, 0].astype(jnp.float32)
    first_imag = first[:, 1].astype(jnp.float32)
    second_real = second[:, 0].astype(jnp.float32)
    second_imag = second[:, 1].astype(jnp.float32)

    def forward_mul(values, matrix):
        return jnp.einsum('rbi,bio->rbo', values, matrix, precision=exact_precision)

    def back_mul(values, matrix):
        return jnp.einsum('rbo,bio->rbi', values, matrix, precision=exact_precision)

    def outer_sum(left, right):
        return jnp.einsum('rbi,rbo->bio', left, right, precision=exact_precision)
    pre_real = forward_mul(spec_real, first_real) - forward_mul(spec_imag, first_imag) + bias[None, :, 0]
    pre_imag = forward_mul(spec_real, first_imag) + forward_mul(spec_imag, first_real) + bias[None, :, 1]
    (act_real, act_imag), backward = jax.vjp(activate, pre_real, pre_imag)
    out_real = error_real * weight_mask[..., None]
    out_imag = error_imag * weight_mask[..., None]
    hid_real = back_mul(out_real, second_real) + back_mul(out_imag, second_imag)
    hid_imag = back_mul(out_imag, second_real) - back_mul(out_real, second_imag)
    grad_real, grad_imag = backward((hid_real, hid_imag))
    in_real = back_mul(grad_real, first_real) + back_mul(grad_imag, first_imag)
    in_imag = back_mul(grad_imag, first_real) - back_mul(grad_real, first_imag)
    second_grad = jnp.stack([outer_sum(act_real, out_real) + outer_sum(act_imag, out_imag), outer_sum(act_real, out_imag) - outer_sum(act_imag, out_real)], axis=1)
    first_grad = jnp.stack([outer_sum(spec_real, grad_real) + outer_sum(spec_imag, grad_imag), outer_sum(spec_real, grad_imag) - outer_sum(spec_imag, grad_real)], axis=1)
    first_bias_grad = jnp.stack([lax.optimization_barrier(jnp.sum(grad_real, axis=0)), lax.optimization_barrier(jnp.sum(grad_imag, axis=0))], axis=1)
    second_bias_grad = jnp.stack([lax.optimization_barrier(jnp.sum(out_real, axis=0)), lax.optimization_barrier(jnp.sum(out_imag, axis=0))], axis=1)
    return (in_real, in_imag, first_grad, second_grad, first_bias_grad, second_bias_grad)

def lat_forward(lat_cos, lat_sin, real_part, imag_part):
    out_real = jnp.einsum('qh,khc->kqc', lat_cos, real_part, precision=exact_precision) + jnp.einsum('qh,khc->kqc', lat_sin, imag_part, precision=exact_precision)
    out_imag = jnp.einsum('qh,khc->kqc', lat_cos, imag_part, precision=exact_precision) - jnp.einsum('qh,khc->kqc', lat_sin, real_part, precision=exact_precision)
    return (out_real, out_imag)

def lat_adjoint(lat_cos, lat_sin, real_part, imag_part):
    out_real = jnp.einsum('qh,kqc->khc', lat_cos, real_part, precision=exact_precision) - jnp.einsum('qh,kqc->khc', lat_sin, imag_part, precision=exact_precision)
    out_imag = jnp.einsum('qh,kqc->khc', lat_sin, real_part, precision=exact_precision) + jnp.einsum('qh,kqc->khc', lat_cos, imag_part, precision=exact_precision)
    return (out_real, out_imag)

def reference(inputs, cotangent, first_weight, first_bias, second_weight, counts, keep_flags):
    modes = jnp.arange(KM, dtype=jnp.int32)
    lon_cos, lon_sin = wave_tables(modes, jnp.arange(W, dtype=jnp.int32), W)
    lat_rows = jnp.arange(H, dtype=jnp.int32)
    lat_cos, lat_sin = wave_tables(lat_rows, lat_rows, H)
    factor = jnp.where(modes == 0, 1.0, 2.0).astype(jnp.float32)[:, None, None]
    field_x = inputs.astype(jnp.float32)
    field_g = cotangent.astype(jnp.float32)
    line_x_real = jnp.einsum('hwc,kw->khc', field_x, lon_cos, precision=exact_precision)
    line_x_imag = -jnp.einsum('hwc,kw->khc', field_x, lon_sin, precision=exact_precision)
    line_g_real = factor * jnp.einsum('hwc,kw->khc', field_g, lon_cos, precision=exact_precision)
    line_g_imag = -factor * jnp.einsum('hwc,kw->khc', field_g, lon_sin, precision=exact_precision)
    spec_real, spec_imag = lat_forward(lat_cos, lat_sin, line_x_real, line_x_imag)
    error_real, error_imag = lat_forward(lat_cos, lat_sin, line_g_real, line_g_imag)
    rows = KM * H
    cut = (modes[:, None] < counts.reshape(NB)[None, :]).astype(jnp.float32)
    flags = jnp.transpose(keep_flags.reshape(H, KM, NB).astype(jnp.float32), (1, 0, 2))
    weight_mask = (cut[:, None, :] * flags).reshape(rows, NB)
    results = mixing_grads(spec_real.reshape(rows, NB, BS), spec_imag.reshape(rows, NB, BS), error_real.reshape(rows, NB, BS), error_imag.reshape(rows, NB, BS), weight_mask, first_weight.reshape(NB, 2, BS, BS), first_bias.reshape(NB, 2, BS), second_weight.reshape(NB, 2, BS, BS))
    in_real, in_imag, first_grad, second_grad, first_bias_grad, second_bias_grad = results
    back_real, back_imag = lat_adjoint(lat_cos, lat_sin, in_real.reshape(KM, H, C), in_imag.reshape(KM, H, C))
    input_grad = jnp.einsum('khc,kw->hwc', back_real, lon_cos, precision=exact_precision) - jnp.einsum('khc,kw->hwc', back_imag, lon_sin, precision=exact_precision)
    return (input_grad.astype(jnp.bfloat16), first_grad.reshape(N_CH, NB // N_CH, 2, BS, BS), second_grad.reshape(N_CH, NB // N_CH, 2, BS, BS), first_bias_grad.reshape(N_CH, NB // N_CH, 2, BS), second_bias_grad.reshape(N_CH, NB // N_CH, 2, BS))
```

```python
import functools
import math

import jax
import jax.numpy as jnp
from jax import lax
from jax.experimental import pallas as pl
from jax.experimental.pallas import tpu as pltpu
from jax.sharding import PartitionSpec as P
import ml_dtypes
import numpy as np

KM = 32


exact_precision = lax.Precision.HIGHEST


def wave_tables(modes, cells, length):
    phase = (modes[:, None] * cells[None, :] % length).astype(jnp.float32)
    angle = phase * (2.0 * math.pi / length)
    scale = 1.0 / math.sqrt(length)
    return (jnp.cos(angle) * scale, jnp.sin(angle) * scale)


def activate(real_part, imag_part):
    return (jax.nn.gelu(real_part, approximate=True), jax.nn.gelu(imag_part, approximate=True))


def mixing_grads(spec_real, spec_imag, error_real, error_imag, weight_mask, first, bias, second):
    first_real = first[:, 0].astype(jnp.float32)
    first_imag = first[:, 1].astype(jnp.float32)
    second_real = second[:, 0].astype(jnp.float32)
    second_imag = second[:, 1].astype(jnp.float32)

    def forward_mul(values, matrix):
        return jnp.einsum("rbi,bio->rbo", values, matrix, precision=exact_precision)

    def back_mul(values, matrix):
        return jnp.einsum("rbo,bio->rbi", values, matrix, precision=exact_precision)

    def outer_sum(left, right):
        return jnp.einsum("rbi,rbo->bio", left, right, precision=exact_precision)

    pre_real = (
        forward_mul(spec_real, first_real) - forward_mul(spec_imag, first_imag) + bias[None, :, 0]
    )
    pre_imag = (
        forward_mul(spec_real, first_imag) + forward_mul(spec_imag, first_real) + bias[None, :, 1]
    )
    (act_real, act_imag), backward = jax.vjp(activate, pre_real, pre_imag)
    out_real = error_real * weight_mask[..., None]
    out_imag = error_imag * weight_mask[..., None]
    hid_real = back_mul(out_real, second_real) + back_mul(out_imag, second_imag)
    hid_imag = back_mul(out_imag, second_real) - back_mul(out_real, second_imag)
    grad_real, grad_imag = backward((hid_real, hid_imag))
    in_real = back_mul(grad_real, first_real) + back_mul(grad_imag, first_imag)
    in_imag = back_mul(grad_imag, first_real) - back_mul(grad_real, first_imag)
    second_grad = jnp.stack(
        [
            outer_sum(act_real, out_real) + outer_sum(act_imag, out_imag),
            outer_sum(act_real, out_imag) - outer_sum(act_imag, out_real),
        ],
        axis=1,
    )
    first_grad = jnp.stack(
        [
            outer_sum(spec_real, grad_real) + outer_sum(spec_imag, grad_imag),
            outer_sum(spec_real, grad_imag) - outer_sum(spec_imag, grad_real),
        ],
        axis=1,
    )
    first_bias_grad = jnp.stack([jnp.sum(grad_real, axis=0), jnp.sum(grad_imag, axis=0)], axis=1)
    second_bias_grad = jnp.stack([jnp.sum(out_real, axis=0), jnp.sum(out_imag, axis=0)], axis=1)
    return (in_real, in_imag, first_grad, second_grad, first_bias_grad, second_bias_grad)


def lat_forward(lat_cos, lat_sin, real_part, imag_part):
    out_real = jnp.einsum(
        "qh,khc->kqc", lat_cos, real_part, precision=exact_precision
    ) + jnp.einsum("qh,khc->kqc", lat_sin, imag_part, precision=exact_precision)
    out_imag = jnp.einsum(
        "qh,khc->kqc", lat_cos, imag_part, precision=exact_precision
    ) - jnp.einsum("qh,khc->kqc", lat_sin, real_part, precision=exact_precision)
    return (out_real, out_imag)


def lat_adjoint(lat_cos, lat_sin, real_part, imag_part):
    out_real = jnp.einsum(
        "qh,kqc->khc", lat_cos, real_part, precision=exact_precision
    ) - jnp.einsum("qh,kqc->khc", lat_sin, imag_part, precision=exact_precision)
    out_imag = jnp.einsum(
        "qh,kqc->khc", lat_sin, real_part, precision=exact_precision
    ) + jnp.einsum("qh,kqc->khc", lat_cos, imag_part, precision=exact_precision)
    return (out_real, out_imag)


def on_device(inputs, cotangent, first_weight, first_bias, second_weight, counts, keep_flags):
    lat_rows, lon_cells, chan_local = inputs.shape
    lon_count = lax.axis_size("lon")
    lat_count = lax.axis_size("lat")
    lon_place = lax.axis_index("lon")
    modes_dev = KM // lon_count
    lon_total = lon_cells * lon_count
    lat_total = lat_rows * lat_count
    own_cells = lon_place * lon_cells + jnp.arange(lon_cells, dtype=jnp.int32)
    own_modes = lon_place * modes_dev + jnp.arange(modes_dev, dtype=jnp.int32)
    field_x = inputs.astype(jnp.float32)
    field_g = cotangent.astype(jnp.float32)
    cosine, sine = wave_tables(
        jnp.arange(modes_dev * lax.axis_size("lon"), dtype=jnp.int32), own_cells, lon_total
    )
    x_real = jnp.einsum("hwc,kw->khc", field_x, cosine, precision=exact_precision)
    x_imag = -jnp.einsum("hwc,kw->khc", field_x, sine, precision=exact_precision)
    g_real = jnp.einsum("hwc,kw->khc", field_g, cosine, precision=exact_precision)
    g_imag = -jnp.einsum("hwc,kw->khc", field_g, sine, precision=exact_precision)
    spectra = lax.psum_scatter(
        jnp.stack([x_real, x_imag, g_real, g_imag], axis=1), "lon", scatter_dimension=0, tiled=True
    )
    factor = jnp.where(own_modes == 0, 1.0, 2.0).astype(jnp.float32)
    unity = jnp.ones_like(factor)
    spectra = spectra * jnp.stack([unity, unity, factor, factor], axis=1)[:, :, None, None]
    blocks = lax.all_to_all(spectra, "lat", split_axis=3, concat_axis=2, tiled=True)
    chan_block = blocks.shape[3]
    block_size = first_weight.shape[-1]
    local_blocks = chan_block // block_size
    lat_index = jnp.arange(lat_total, dtype=jnp.int32)
    lat_cos, lat_sin = wave_tables(lat_index, lat_index, lat_total)
    spec_real, spec_imag = lat_forward(lat_cos, lat_sin, blocks[:, 0], blocks[:, 1])
    error_real, error_imag = lat_forward(lat_cos, lat_sin, blocks[:, 2], blocks[:, 3])
    rows = modes_dev * lat_total
    cut = (own_modes[:, None] < counts[0][None, :]).astype(jnp.float32)
    flags = jnp.transpose(keep_flags[:, :, 0, :].astype(jnp.float32), (1, 0, 2))
    weight_mask = (cut[:, None, :] * flags).reshape(rows, local_blocks)

    def as_rows(values):
        return values.reshape(rows, local_blocks, block_size)

    results = mixing_grads(
        as_rows(spec_real),
        as_rows(spec_imag),
        as_rows(error_real),
        as_rows(error_imag),
        weight_mask,
        first_weight[0],
        first_bias[0],
        second_weight[0],
    )
    in_real, in_imag, first_grad, second_grad, first_bias_grad, second_bias_grad = results
    first_grad, second_grad, first_bias_grad, second_bias_grad = lax.psum(
        (first_grad, second_grad, first_bias_grad, second_bias_grad), "lon"
    )
    back_real, back_imag = lat_adjoint(
        lat_cos,
        lat_sin,
        in_real.reshape(modes_dev, lat_total, chan_block),
        in_imag.reshape(modes_dev, lat_total, chan_block),
    )
    back = lax.all_to_all(
        jnp.stack([back_real, back_imag], axis=1), "lat", split_axis=2, concat_axis=3, tiled=True
    )
    piece = lax.all_gather(back, "lon", axis=0, tiled=True)
    cosine, sine = wave_tables(jnp.arange(piece.shape[0], dtype=jnp.int32), own_cells, lon_total)
    total = jnp.einsum("khc,kw->hwc", piece[:, 0], cosine, precision=exact_precision)
    input_grad = (
        total - jnp.einsum("khc,kw->hwc", piece[:, 1], sine, precision=exact_precision)
    ).astype(jnp.bfloat16)
    return (
        input_grad,
        first_grad[None],
        second_grad[None],
        first_bias_grad[None],
        second_bias_grad[None],
    )


MESH = pl.DeviceIdType.MESH
TOP = 32767.0
LEAST = 1e-30


def np_split(table):
    high = table.astype(ml_dtypes.bfloat16)
    low = (table - high.astype(np.float64)).astype(ml_dtypes.bfloat16)
    return high, low


def split(values):
    high = values.astype(jnp.bfloat16)
    low = (values - high.astype(jnp.float32)).astype(jnp.bfloat16)
    return high, low


def np_waves(modes, cells, length):
    angle = (modes[:, None] * cells[None, :] % length) * (2.0 * np.pi / length)
    return np.cos(angle) / np.sqrt(length), np.sin(angle) / np.sqrt(length)


def lon_table(length):
    cosine, sine = np_waves(np.arange(KM), np.arange(length), length)
    return np.stack([cosine, -sine], axis=1).reshape(2 * KM, length)


def lat_tables(length, modes):
    index = np.arange(length)
    cosine, sine = np_waves(index, index, length)
    there = np.zeros((2, 2, modes, length, length, 2, modes, 2))
    back = np.zeros((length, modes, 2, 2, modes, length))
    for k in range(modes):
        for f in range(2):
            there[f, 0, k, :, :, f, k, 0] = cosine
            there[f, 0, k, :, :, f, k, 1] = sine
            there[f, 1, k, :, :, f, k, 1] = cosine
            there[f, 1, k, :, :, f, k, 0] = -sine
        back[:, k, 0, 0, k, :] = cosine.T
        back[:, k, 0, 1, k, :] = -sine.T
        back[:, k, 1, 0, k, :] = sine.T
        back[:, k, 1, 1, k, :] = cosine.T
    rows = 4 * modes * length
    return there.reshape(rows, rows), back.reshape(rows // 2, rows // 2)


def dot(left, right, dims=((1,), (0,))):
    return lax.dot_general(left, right, (dims, ((), ())), preferred_element_type=jnp.float32)


def dot_exact_right(left, right, dims=((1,), (0,))):
    high, low = split(left)
    return dot(high, right, dims) + dot(low, right, dims)


def dot_both(left, right, dims=((1,), (0,))):
    left_high, left_low = left
    right_high, right_low = right
    return (
        dot(left_high, right_high, dims)
        + dot(left_high, right_low, dims)
        + dot(left_low, right_high, dims)
    )


def code(values):
    most = jnp.maximum(jnp.max(jnp.abs(values), axis=1, keepdims=True), LEAST)
    return jnp.round(values * (TOP / most)).astype(jnp.int32), most * (1.0 / TOP)


def pick(scales, lane):
    lanes = lax.broadcasted_iota(jnp.int32, scales.shape, scales.ndim - 1)
    return jnp.sum(jnp.where(lanes == lane, scales, 0.0), axis=-1, keepdims=True)


def place(lat_count):
    return lax.axis_index("lon") * lat_count + lax.axis_index("lat")


def device(number, lat_count):
    return {"lon": lax.div(number, lat_count), "lat": lax.rem(number, lat_count)}


def greet(group, lat_count):
    me = place(lat_count)
    barrier = pltpu.get_barrier_semaphore()
    for step in range(1, group):
        pl.semaphore_signal(
            barrier,
            inc=1,
            device_id=device(lax.rem(me + step, group), lat_count),
            device_id_type=MESH,
        )
    pl.semaphore_wait(barrier, group - 1)


def forward_kernel(
    group, lat_count, chunks, table_ref, factor_ref, x_ref, g_ref, sums_ref, scales_ref,
    send, scales, send_sem, recv_sem, own_sem, scale_send_sem, scale_recv_sem, scale_own_sem,
):
    step_now = pl.program_id(0)
    me = place(lat_count)
    per_chunk = x_ref.shape[0]
    rows = table_ref.shape[0] // 2
    own = rows // group

    def sums_copy(chunk, step, arriving):
        target = lax.rem(me + step, group)
        slot = lax.rem(me + group - step, group) if arriving else me
        here = pl.ds(chunk * per_chunk, per_chunk)
        return pltpu.make_async_remote_copy(
            src_ref=send.at[target, here],
            dst_ref=sums_ref.at[slot, here],
            send_sem=send_sem.at[chunk, step],
            recv_sem=recv_sem.at[chunk, step],
            device_id=device(target, lat_count),
            device_id_type=MESH,
        )

    def own_copy(chunk):
        here = pl.ds(chunk * per_chunk, per_chunk)
        return pltpu.make_async_copy(send.at[me, here], sums_ref.at[me, here], own_sem.at[chunk])

    def scales_copy(step, arriving):
        target = lax.rem(me + step, group)
        slot = lax.rem(me + group - step, group) if arriving else me
        return pltpu.make_async_remote_copy(
            src_ref=scales.at[target],
            dst_ref=scales_ref.at[slot],
            send_sem=scale_send_sem.at[step],
            recv_sem=scale_recv_sem.at[step],
            device_id=device(target, lat_count),
            device_id_type=MESH,
        )

    @pl.when(step_now == 0)
    def _():
        greet(group, lat_count)
        scales[...] = jnp.zeros_like(scales)

    table = table_ref[...]
    lanes = lax.broadcasted_iota(jnp.int32, (own, 128), 1)
    for inside in range(per_chunk):
        h = step_now * per_chunk + inside
        both_x = dot(table, x_ref[inside])
        both_g = dot(table, g_ref[inside])
        coded_x, scale_x = code(both_x[:rows] + both_x[rows:])
        coded_g, scale_g = code(both_g[:rows] + both_g[rows:])
        scale_g = scale_g * factor_ref[...]
        for target in range(group):
            at = slice(target * own, (target + 1) * own)
            send[target, h] = jnp.concatenate([coded_x[at], coded_g[at]], axis=0).astype(jnp.int16)
            scales[target, 0:own] = jnp.where(lanes == h, scale_x[at], scales[target, 0:own])
            scales[target, own : 2 * own] = jnp.where(
                lanes == h, scale_g[at], scales[target, own : 2 * own]
            )
    for step in range(1, group):
        sums_copy(step_now, step, False).start()
    own_copy(step_now).start()

    @pl.when(step_now == chunks - 1)
    def _():
        for step in range(1, group):
            scales_copy(step, False).start()
        scale_own = pltpu.make_async_copy(scales.at[me], scales_ref.at[me], scale_own_sem)
        scale_own.start()

        def finish(chunk, carry):
            for step in range(1, group):
                sums_copy(chunk, step, False).wait_send()
                sums_copy(chunk, step, True).wait_recv()
            own_copy(chunk).wait()
            return carry

        lax.fori_loop(0, chunks, finish, 0)
        for step in range(1, group):
            scales_copy(step, False).wait_send()
            scales_copy(step, True).wait_recv()
        scale_own.wait()


def gelu_and_slope(values):
    root = math.sqrt(2.0 / math.pi)
    square = values * values
    tanh = jnp.tanh(root * (values + 0.044715 * (square * values)))
    half = 0.5 * (1.0 + tanh)
    slope = half + 0.5 * values * (1.0 - tanh * tanh) * (root * (1.0 + 3.0 * 0.044715 * square))
    return values * half, slope


def spectral_kernel(
    group, lat_count, sums_ref, scales_ref, there_high, there_low, back_high, back_low,
    first_ref, second_ref, bias_ref, mask_ref,
    coded_ref, coded_scales_ref, first_grad_ref, second_grad_ref, bias_grad_ref,
    line, send, scales, send_sem, recv_sem, own_sem, scale_send_sem, scale_recv_sem, scale_own_sem,
):
    me = place(lat_count)
    lon_count = group // lat_count
    lat_rows, mode_rows, chans = sums_ref.shape[1:]
    greet(group, lat_count)

    def gather(h, carry):
        for part in range(lat_count):
            total = None
            for lon in range(lon_count):
                source = lon * lat_count + part
                term = sums_ref[source, h].astype(jnp.int32).astype(jnp.float32) * pick(
                    scales_ref[source], h
                )
                total = term if total is None else total + term
            start = pl.multiple_of((part * lat_rows + h) * mode_rows, mode_rows)
            line[pl.ds(start, mode_rows), :] = total
        return carry

    lax.fori_loop(0, lat_rows, gather, 0)
    fields = dot_both((there_high[...], there_low[...]), split(line[...]))
    rows = fields.shape[0] // 4
    mask = mask_ref[...]
    spec = jnp.concatenate([fields[:rows], fields[rows : 2 * rows]], axis=1)
    out = jnp.concatenate(
        [fields[2 * rows : 3 * rows] * mask, fields[3 * rows :] * mask], axis=1
    )
    turned = ((1,), (1,))
    pre = dot_exact_right(spec, first_ref[...]) + bias_ref[...]
    act, slope = gelu_and_slope(pre)
    pre_grad = dot_exact_right(out, second_ref[...], turned) * slope
    spec_grad = dot_exact_right(pre_grad, first_ref[...], turned)
    spec_grad = jnp.concatenate([spec_grad[:, :chans], spec_grad[:, chans:]], axis=0)
    back = dot_both((back_high[...], back_low[...]), split(spec_grad))
    coded, scale = code(back)
    pairs = send.shape[1]
    send[...] = coded.astype(jnp.int16).reshape(send.shape)
    lanes = lax.broadcasted_iota(jnp.int32, (16, 128), 1)
    for part in range(lat_count):
        packed = jnp.zeros((16, 128), jnp.float32)
        for pair in range(pairs):
            start = (part * pairs + pair) * 16
            packed = jnp.where(lanes == pair, scale[start : start + 16], packed)
        scales[part] = packed

    def copies(step, arriving):
        target = lax.rem(me + step, group)
        part = lax.rem(target, lat_count)
        slot = lax.rem(me + group - step, group) if arriving else me
        return [
            pltpu.make_async_remote_copy(
                src_ref=source.at[part],
                dst_ref=landing.at[slot],
                send_sem=sent.at[step],
                recv_sem=arrived.at[step],
                device_id=device(target, lat_count),
                device_id_type=MESH,
            )
            for source, landing, sent, arrived in (
                (send, coded_ref, send_sem, recv_sem),
                (scales, coded_scales_ref, scale_send_sem, scale_recv_sem),
            )
        ]

    for step in range(1, group):
        for copy in copies(step, False):
            copy.start()
    my_part = lax.axis_index("lat")
    own = pltpu.make_async_copy(send.at[my_part], coded_ref.at[me], own_sem)
    own_scale = pltpu.make_async_copy(scales.at[my_part], coded_scales_ref.at[me], scale_own_sem)
    own.start()
    own_scale.start()

    def weight_grad(left, right):
        left = jnp.concatenate([left[:, :chans], left[:, chans:]], axis=0)
        right_real, right_imag = right[:, :chans], right[:, chans:]
        right = jnp.concatenate(
            [
                jnp.concatenate([right_real, right_imag], axis=1),
                jnp.concatenate([right_imag, -right_real], axis=1),
            ],
            axis=0,
        )
        return dot_both(split(left), split(right), ((0,), (0,)))

    first_grad_ref[...] = weight_grad(spec, pre_grad)
    second_grad_ref[...] = weight_grad(act, out)
    bias_grad_ref[0:1] = jnp.sum(pre_grad, axis=0, keepdims=True)
    bias_grad_ref[1:2] = jnp.sum(out, axis=0, keepdims=True)
    for step in range(1, group):
        for copy in copies(step, False):
            copy.wait_send()
        for copy in copies(step, True):
            copy.wait_recv()
    own.wait()
    own_scale.wait()


def inverse_kernel(table_ref, coded_ref, scales_ref, out_ref):
    scale = pick(scales_ref[...], pl.program_id(0))
    values = coded_ref[:, 0].astype(jnp.int32).astype(jnp.float32) * scale
    group, rows, chans = values.shape
    for inside in range(2):
        part = values[:, inside * rows // 2 : (inside + 1) * rows // 2].reshape(
            group * rows // 2, chans
        )
        high, low = split(part)
        out_ref[inside] = dot(
            table_ref[...], jnp.concatenate([high, low, high], axis=0)
        ).astype(jnp.bfloat16)


def block_diagonal(weights):
    blocks, _, size, _ = weights.shape

    def spread(part):
        eye = jnp.eye(blocks, dtype=part.dtype)
        full = part[:, :, None, :] * eye[:, None, :, None]
        return full.reshape(blocks * size, blocks * size)

    real, imag = spread(weights[:, 0]), spread(weights[:, 1])
    return jnp.concatenate(
        [jnp.concatenate([real, imag], axis=1), jnp.concatenate([-imag, real], axis=1)], axis=0
    )


def diagonal_blocks(grad, blocks, size):
    whole = grad.reshape(blocks, size, 2, blocks, size)
    return jnp.stack([jnp.swapaxes(whole[b, :, :, b], 0, 1) for b in range(blocks)])


def on_device_coded(
    inputs, cotangent, first_weight, first_bias, second_weight, counts, keep_flags
):
    lat_rows, lon_cells, chans = inputs.shape
    lon_count, lat_count = lax.axis_size("lon"), lax.axis_size("lat")
    lon_place, lat_place = lax.axis_index("lon"), lax.axis_index("lat")
    group = lon_count * lat_count
    modes_lon = KM // lon_count
    modes_own = KM // group
    lat_total = lat_rows * lat_count
    mine = first_weight.shape[1]
    size = first_weight.shape[-1]
    blocks = mine * lat_count
    vmem = pl.BlockSpec(memory_space=pltpu.VMEM)
    hbm = pl.BlockSpec(memory_space=pl.ANY)

    lon_high, lon_low = np_split(lon_table(lon_cells * lon_count))
    table = np.concatenate([lon_high, lon_low], axis=0)
    table = table.reshape(4 * KM, lon_count, lon_cells).transpose(1, 0, 2)
    table = lax.dynamic_index_in_dim(jnp.asarray(table), lon_place, 0, keepdims=False)
    table_back = np.concatenate([lon_high, lon_high, lon_low], axis=0).T
    table_back = table_back.reshape(lon_count, lon_cells, 6 * KM)
    table_back = lax.dynamic_index_in_dim(jnp.asarray(table_back), lon_place, 0, keepdims=False)
    there, back = lat_tables(lat_total, modes_own)
    factor = np.full((2 * KM, 1), 2.0, np.float32)
    factor[:2] = 1.0

    own_modes = lon_place * modes_lon + jnp.arange(modes_lon, dtype=jnp.int32)
    cut = own_modes[:, None] < counts[0][None, :]
    mask = jnp.where(cut[None], keep_flags[:, :, 0, :].astype(jnp.float32), 0.0)
    small = jnp.concatenate([mask.reshape(-1), first_bias.reshape(-1)])
    small = lax.all_gather(small, "lat", axis=0)
    weights = lax.all_gather(jnp.stack([first_weight[0], second_weight[0]]), "lat", axis=1, tiled=True)
    mask = small[:, : mask.size].reshape(lat_count, lat_total, modes_lon, mine)
    mask = lax.dynamic_slice_in_dim(mask, lat_place * modes_own, modes_own, 2)
    mask = jnp.transpose(mask, (2, 1, 0, 3)).reshape(modes_own * lat_total, blocks)
    mask = jnp.repeat(mask, size, axis=1)
    bias = small[:, -first_bias.size :].reshape(blocks, 2, size)
    bias = jnp.transpose(bias, (1, 0, 2)).reshape(1, 2 * chans)
    first, second = block_diagonal(weights[0]), block_diagonal(weights[1])

    per_chunk = 4
    chunks = lat_rows // per_chunk
    rows = 4 * modes_own
    dma = pltpu.SemaphoreType.DMA
    block = pl.BlockSpec((per_chunk, lon_cells, chans), lambda i: (i, 0, 0))
    sums, scales = pl.pallas_call(
        functools.partial(forward_kernel, group, lat_count, chunks),
        grid=(chunks,),
        out_shape=(
            jax.ShapeDtypeStruct((group, lat_rows, rows, chans), jnp.int16),
            jax.ShapeDtypeStruct((group, rows, 128), jnp.float32),
        ),
        in_specs=[
            pl.BlockSpec(table.shape, lambda i: (0, 0)),
            pl.BlockSpec(factor.shape, lambda i: (0, 0)),
            block,
            block,
        ],
        out_specs=(hbm, hbm),
        scratch_shapes=[
            pltpu.VMEM((group, lat_rows, rows, chans), jnp.int16),
            pltpu.VMEM((group, rows, 128), jnp.float32),
            dma((chunks, group)),
            dma((chunks, group)),
            dma((chunks,)),
            dma((group,)),
            dma((group,)),
            dma,
        ],
        compiler_params=pltpu.CompilerParams(
            collective_id=0, has_side_effects=True, vmem_limit_bytes=40 * 2**20
        ),
        cost_estimate=pl.CostEstimate(
            flops=16 * KM * inputs.size, bytes_accessed=4 * inputs.size, transcendentals=0
        ),
    )(table, jnp.asarray(factor), inputs, cotangent)

    pairs = lat_rows // 2
    coded, coded_scales, first_grad, second_grad, bias_grad = pl.pallas_call(
        functools.partial(spectral_kernel, group, lat_count),
        out_shape=(
            jax.ShapeDtypeStruct((group, pairs, 4 * modes_own, chans), jnp.int16),
            jax.ShapeDtypeStruct((group, 16, 128), jnp.float32),
            jax.ShapeDtypeStruct((chans, 2 * chans), jnp.float32),
            jax.ShapeDtypeStruct((chans, 2 * chans), jnp.float32),
            jax.ShapeDtypeStruct((2, 2 * chans), jnp.float32),
        ),
        in_specs=[vmem] * 10,
        out_specs=(hbm, hbm, vmem, vmem, vmem),
        scratch_shapes=[
            pltpu.VMEM((4 * modes_own * lat_total, chans), jnp.float32),
            pltpu.VMEM((lat_count, pairs, 4 * modes_own, chans), jnp.int16),
            pltpu.VMEM((lat_count, 16, 128), jnp.float32),
            dma((group,)),
            dma((group,)),
            dma,
            dma((group,)),
            dma((group,)),
            dma,
        ],
        compiler_params=pltpu.CompilerParams(
            collective_id=1, has_side_effects=True, vmem_limit_bytes=56 * 2**20
        ),
    )(
        sums,
        scales,
        *(jnp.asarray(part) for part in np_split(there)),
        *(jnp.asarray(part) for part in np_split(back)),
        first,
        second,
        bias,
        mask,
    )

    grads = jnp.stack(
        [diagonal_blocks(first_grad, blocks, size), diagonal_blocks(second_grad, blocks, size)]
    )
    bias_grads = jnp.transpose(bias_grad.reshape(2, 2, blocks, size), (0, 2, 1, 3))
    grads = jnp.concatenate([grads, bias_grads[:, :, :, None, :]], axis=3)
    grads = lax.psum(grads, ("lon", "lat"))
    grads = lax.dynamic_slice_in_dim(grads, lat_place * mine, mine, 1)

    input_grad = pl.pallas_call(
        inverse_kernel,
        grid=(pairs,),
        out_shape=jax.ShapeDtypeStruct(inputs.shape, jnp.bfloat16),
        in_specs=[
            pl.BlockSpec(table_back.shape, lambda i: (0, 0)),
            pl.BlockSpec((group, 1, 4 * modes_own, chans), lambda i: (0, i, 0, 0)),
            pl.BlockSpec((group, 16, 128), lambda i: (0, 0, 0)),
        ],
        out_specs=pl.BlockSpec((2, lon_cells, chans), lambda i: (i, 0, 0)),
        compiler_params=pltpu.CompilerParams(vmem_limit_bytes=32 * 2**20),
        cost_estimate=pl.CostEstimate(
            flops=12 * KM * inputs.size, bytes_accessed=2 * inputs.size, transcendentals=0
        ),
    )(table_back, coded, coded_scales)
    return (
        input_grad,
        grads[0][None, :, :, :size],
        grads[1][None, :, :, :size],
        grads[0][None, :, :, size],
        grads[1][None, :, :, size],
    )


def solution(mesh):
    group = mesh.shape["lon"] * mesh.shape["lat"]
    body = on_device_coded if KM == 4 * group else on_device
    return jax.shard_map(
        body,
        mesh=mesh,
        in_specs=(
            P(("ens", "lat"), "lon", "ch"),
            P(("ens", "lat"), "lon", "ch"),
            P("ch", "lat", None, None, None),
            P("ch", "lat", None, None),
            P("ch", "lat", None, None, None),
            P("ch", "lat"),
            P(None, "lon", "ch", "lat"),
        ),
        out_specs=(
            P(("ens", "lat"), "lon", "ch"),
            P(("ens", "ch"), "lat", None, None, None),
            P(("ens", "ch"), "lat", None, None, None),
            P(("ens", "ch"), "lat", None, None),
            P(("ens", "ch"), "lat", None, None),
        ),
        check_vma=False,
    )
```

```python
import functools
import math

import jax
import jax.numpy as jnp
from jax import lax
from jax.experimental import pallas as pl
from jax.experimental.pallas import tpu as pltpu
from jax.sharding import PartitionSpec as P
import ml_dtypes
import numpy as np

KM = 32


exact_precision = lax.Precision.HIGHEST


def wave_tables(modes, cells, length):
    phase = (modes[:, None] * cells[None, :] % length).astype(jnp.float32)
    angle = phase * (2.0 * math.pi / length)
    scale = 1.0 / math.sqrt(length)
    return (jnp.cos(angle) * scale, jnp.sin(angle) * scale)


def activate(real_part, imag_part):
    return (jax.nn.gelu(real_part, approximate=True), jax.nn.gelu(imag_part, approximate=True))


def mixing_grads(spec_real, spec_imag, error_real, error_imag, weight_mask, first, bias, second):
    first_real = first[:, 0].astype(jnp.float32)
    first_imag = first[:, 1].astype(jnp.float32)
    second_real = second[:, 0].astype(jnp.float32)
    second_imag = second[:, 1].astype(jnp.float32)

    def forward_mul(values, matrix):
        return jnp.einsum("rbi,bio->rbo", values, matrix, precision=exact_precision)

    def back_mul(values, matrix):
        return jnp.einsum("rbo,bio->rbi", values, matrix, precision=exact_precision)

    def outer_sum(left, right):
        return jnp.einsum("rbi,rbo->bio", left, right, precision=exact_precision)

    pre_real = (
        forward_mul(spec_real, first_real) - forward_mul(spec_imag, first_imag) + bias[None, :, 0]
    )
    pre_imag = (
        forward_mul(spec_real, first_imag) + forward_mul(spec_imag, first_real) + bias[None, :, 1]
    )
    (act_real, act_imag), backward = jax.vjp(activate, pre_real, pre_imag)
    out_real = error_real * weight_mask[..., None]
    out_imag = error_imag * weight_mask[..., None]
    hid_real = back_mul(out_real, second_real) + back_mul(out_imag, second_imag)
    hid_imag = back_mul(out_imag, second_real) - back_mul(out_real, second_imag)
    grad_real, grad_imag = backward((hid_real, hid_imag))
    in_real = back_mul(grad_real, first_real) + back_mul(grad_imag, first_imag)
    in_imag = back_mul(grad_imag, first_real) - back_mul(grad_real, first_imag)
    second_grad = jnp.stack(
        [
            outer_sum(act_real, out_real) + outer_sum(act_imag, out_imag),
            outer_sum(act_real, out_imag) - outer_sum(act_imag, out_real),
        ],
        axis=1,
    )
    first_grad = jnp.stack(
        [
            outer_sum(spec_real, grad_real) + outer_sum(spec_imag, grad_imag),
            outer_sum(spec_real, grad_imag) - outer_sum(spec_imag, grad_real),
        ],
        axis=1,
    )
    first_bias_grad = jnp.stack([jnp.sum(grad_real, axis=0), jnp.sum(grad_imag, axis=0)], axis=1)
    second_bias_grad = jnp.stack([jnp.sum(out_real, axis=0), jnp.sum(out_imag, axis=0)], axis=1)
    return (in_real, in_imag, first_grad, second_grad, first_bias_grad, second_bias_grad)


def lat_forward(lat_cos, lat_sin, real_part, imag_part):
    out_real = jnp.einsum(
        "qh,khc->kqc", lat_cos, real_part, precision=exact_precision
    ) + jnp.einsum("qh,khc->kqc", lat_sin, imag_part, precision=exact_precision)
    out_imag = jnp.einsum(
        "qh,khc->kqc", lat_cos, imag_part, precision=exact_precision
    ) - jnp.einsum("qh,khc->kqc", lat_sin, real_part, precision=exact_precision)
    return (out_real, out_imag)


def lat_adjoint(lat_cos, lat_sin, real_part, imag_part):
    out_real = jnp.einsum(
        "qh,kqc->khc", lat_cos, real_part, precision=exact_precision
    ) - jnp.einsum("qh,kqc->khc", lat_sin, imag_part, precision=exact_precision)
    out_imag = jnp.einsum(
        "qh,kqc->khc", lat_sin, real_part, precision=exact_precision
    ) + jnp.einsum("qh,kqc->khc", lat_cos, imag_part, precision=exact_precision)
    return (out_real, out_imag)


def on_device(inputs, cotangent, first_weight, first_bias, second_weight, counts, keep_flags):
    lat_rows, lon_cells, chan_local = inputs.shape
    lon_count = lax.axis_size("lon")
    lat_count = lax.axis_size("lat")
    lon_place = lax.axis_index("lon")
    modes_dev = KM // lon_count
    lon_total = lon_cells * lon_count
    lat_total = lat_rows * lat_count
    own_cells = lon_place * lon_cells + jnp.arange(lon_cells, dtype=jnp.int32)
    own_modes = lon_place * modes_dev + jnp.arange(modes_dev, dtype=jnp.int32)
    field_x = inputs.astype(jnp.float32)
    field_g = cotangent.astype(jnp.float32)
    cosine, sine = wave_tables(
        jnp.arange(modes_dev * lax.axis_size("lon"), dtype=jnp.int32), own_cells, lon_total
    )
    x_real = jnp.einsum("hwc,kw->khc", field_x, cosine, precision=exact_precision)
    x_imag = -jnp.einsum("hwc,kw->khc", field_x, sine, precision=exact_precision)
    g_real = jnp.einsum("hwc,kw->khc", field_g, cosine, precision=exact_precision)
    g_imag = -jnp.einsum("hwc,kw->khc", field_g, sine, precision=exact_precision)
    spectra = lax.psum_scatter(
        jnp.stack([x_real, x_imag, g_real, g_imag], axis=1), "lon", scatter_dimension=0, tiled=True
    )
    factor = jnp.where(own_modes == 0, 1.0, 2.0).astype(jnp.float32)
    unity = jnp.ones_like(factor)
    spectra = spectra * jnp.stack([unity, unity, factor, factor], axis=1)[:, :, None, None]
    blocks = lax.all_to_all(spectra, "lat", split_axis=3, concat_axis=2, tiled=True)
    chan_block = blocks.shape[3]
    block_size = first_weight.shape[-1]
    local_blocks = chan_block // block_size
    lat_index = jnp.arange(lat_total, dtype=jnp.int32)
    lat_cos, lat_sin = wave_tables(lat_index, lat_index, lat_total)
    spec_real, spec_imag = lat_forward(lat_cos, lat_sin, blocks[:, 0], blocks[:, 1])
    error_real, error_imag = lat_forward(lat_cos, lat_sin, blocks[:, 2], blocks[:, 3])
    rows = modes_dev * lat_total
    cut = (own_modes[:, None] < counts[0][None, :]).astype(jnp.float32)
    flags = jnp.transpose(keep_flags[:, :, 0, :].astype(jnp.float32), (1, 0, 2))
    weight_mask = (cut[:, None, :] * flags).reshape(rows, local_blocks)

    def as_rows(values):
        return values.reshape(rows, local_blocks, block_size)

    results = mixing_grads(
        as_rows(spec_real),
        as_rows(spec_imag),
        as_rows(error_real),
        as_rows(error_imag),
        weight_mask,
        first_weight[0],
        first_bias[0],
        second_weight[0],
    )
    in_real, in_imag, first_grad, second_grad, first_bias_grad, second_bias_grad = results
    first_grad, second_grad, first_bias_grad, second_bias_grad = lax.psum(
        (first_grad, second_grad, first_bias_grad, second_bias_grad), "lon"
    )
    back_real, back_imag = lat_adjoint(
        lat_cos,
        lat_sin,
        in_real.reshape(modes_dev, lat_total, chan_block),
        in_imag.reshape(modes_dev, lat_total, chan_block),
    )
    back = lax.all_to_all(
        jnp.stack([back_real, back_imag], axis=1), "lat", split_axis=2, concat_axis=3, tiled=True
    )
    piece = lax.all_gather(back, "lon", axis=0, tiled=True)
    cosine, sine = wave_tables(jnp.arange(piece.shape[0], dtype=jnp.int32), own_cells, lon_total)
    total = jnp.einsum("khc,kw->hwc", piece[:, 0], cosine, precision=exact_precision)
    input_grad = (
        total - jnp.einsum("khc,kw->hwc", piece[:, 1], sine, precision=exact_precision)
    ).astype(jnp.bfloat16)
    return (
        input_grad,
        first_grad[None],
        second_grad[None],
        first_bias_grad[None],
        second_bias_grad[None],
    )


MESH = pl.DeviceIdType.MESH
TOP = 32767.0
LEAST = 1e-30


def np_split(table):
    high = table.astype(ml_dtypes.bfloat16)
    low = (table - high.astype(np.float64)).astype(ml_dtypes.bfloat16)
    return high, low


def split(values):
    high = values.astype(jnp.bfloat16)
    low = (values - high.astype(jnp.float32)).astype(jnp.bfloat16)
    return high, low


def np_waves(modes, cells, length):
    angle = (modes[:, None] * cells[None, :] % length) * (2.0 * np.pi / length)
    return np.cos(angle) / np.sqrt(length), np.sin(angle) / np.sqrt(length)


def lon_table(length):
    cosine, sine = np_waves(np.arange(KM), np.arange(length), length)
    return np.stack([cosine, -sine], axis=1).reshape(2 * KM, length)


def lat_tables(length, modes):
    index = np.arange(length)
    cosine, sine = np_waves(index, index, length)
    there = np.zeros((2, 2, modes, length, length, 2, modes, 2))
    back = np.zeros((length, modes, 2, 2, modes, length))
    for k in range(modes):
        for f in range(2):
            there[f, 0, k, :, :, f, k, 0] = cosine
            there[f, 0, k, :, :, f, k, 1] = sine
            there[f, 1, k, :, :, f, k, 1] = cosine
            there[f, 1, k, :, :, f, k, 0] = -sine
        back[:, k, 0, 0, k, :] = cosine.T
        back[:, k, 0, 1, k, :] = -sine.T
        back[:, k, 1, 0, k, :] = sine.T
        back[:, k, 1, 1, k, :] = cosine.T
    rows = 4 * modes * length
    return there.reshape(rows, rows), back.reshape(rows // 2, rows // 2)


def dot(left, right, dims=((1,), (0,))):
    return lax.dot_general(left, right, (dims, ((), ())), preferred_element_type=jnp.float32)


def dot_exact_right(left, right, dims=((1,), (0,))):
    high, low = split(left)
    return dot(high, right, dims) + dot(low, right, dims)


def dot_both(left, right, dims=((1,), (0,))):
    left_high, left_low = left
    right_high, right_low = right
    return (
        dot(left_high, right_high, dims)
        + dot(left_high, right_low, dims)
        + dot(left_low, right_high, dims)
    )


def code(values):
    most = jnp.maximum(jnp.max(jnp.abs(values), axis=1, keepdims=True), LEAST)
    return jnp.round(values * (TOP / most)).astype(jnp.int32), most * (1.0 / TOP)


def pick(scales, lane):
    lanes = lax.broadcasted_iota(jnp.int32, scales.shape, scales.ndim - 1)
    return jnp.sum(jnp.where(lanes == lane, scales, 0.0), axis=-1, keepdims=True)


def place(lat_count):
    return lax.axis_index("lon") * lat_count + lax.axis_index("lat")


def device(number, lat_count):
    return {"lon": lax.div(number, lat_count), "lat": lax.rem(number, lat_count)}


def greet(group, lat_count):
    me = place(lat_count)
    barrier = pltpu.get_barrier_semaphore()
    for step in range(1, group):
        pl.semaphore_signal(
            barrier,
            inc=1,
            device_id=device(lax.rem(me + step, group), lat_count),
            device_id_type=MESH,
        )
    pl.semaphore_wait(barrier, group - 1)


def forward_kernel(
    group, lat_count, chunks, table_ref, factor_ref, weights_ref, small_ref, x_ref, g_ref,
    sums_ref, scales_ref, all_weights_ref, all_small_ref,
    send, scales, send_sem, recv_sem, own_sem, scale_send_sem, scale_recv_sem, scale_own_sem,
    side_send_sem, side_recv_sem, side_own_sem,
):
    step_now = pl.program_id(0)
    me = place(lat_count)
    per_chunk = x_ref.shape[0]
    rows = table_ref.shape[0] // 2
    own = rows // group

    def sums_copy(chunk, step, arriving):
        target = lax.rem(me + step, group)
        slot = lax.rem(me + group - step, group) if arriving else me
        here = pl.ds(chunk * per_chunk, per_chunk)
        return pltpu.make_async_remote_copy(
            src_ref=send.at[target, here],
            dst_ref=sums_ref.at[slot, here],
            send_sem=send_sem.at[chunk, step],
            recv_sem=recv_sem.at[chunk, step],
            device_id=device(target, lat_count),
            device_id_type=MESH,
        )

    def own_copy(chunk):
        here = pl.ds(chunk * per_chunk, per_chunk)
        return pltpu.make_async_copy(send.at[me, here], sums_ref.at[me, here], own_sem.at[chunk])

    def scales_copy(step, arriving):
        target = lax.rem(me + step, group)
        slot = lax.rem(me + group - step, group) if arriving else me
        return pltpu.make_async_remote_copy(
            src_ref=scales.at[target],
            dst_ref=scales_ref.at[slot],
            send_sem=scale_send_sem.at[step],
            recv_sem=scale_recv_sem.at[step],
            device_id=device(target, lat_count),
            device_id_type=MESH,
        )

    sides = ((weights_ref, all_weights_ref), (small_ref, all_small_ref))
    my_part = lax.axis_index("lat")

    def side_copies(step, arriving):
        target = lax.rem(my_part + step, lat_count)
        slot = lax.rem(my_part + lat_count - step, lat_count) if arriving else my_part
        return [
            pltpu.make_async_remote_copy(
                src_ref=source,
                dst_ref=landing.at[slot],
                send_sem=side_send_sem.at[which, step],
                recv_sem=side_recv_sem.at[which, step],
                device_id={"lat": target},
                device_id_type=MESH,
            )
            for which, (source, landing) in enumerate(sides)
        ]

    def side_own():
        return [
            pltpu.make_async_copy(source, landing.at[my_part], side_own_sem.at[which])
            for which, (source, landing) in enumerate(sides)
        ]

    @pl.when(step_now == 0)
    def _():
        greet(group, lat_count)
        for step in range(1, lat_count):
            for copy in side_copies(step, False):
                copy.start()
        for copy in side_own():
            copy.start()
        scales[...] = jnp.zeros_like(scales)

    table = table_ref[...]
    lanes = lax.broadcasted_iota(jnp.int32, (own, 128), 1)
    for inside in range(per_chunk):
        h = step_now * per_chunk + inside
        both_x = dot(table, x_ref[inside])
        both_g = dot(table, g_ref[inside])
        coded_x, scale_x = code(both_x[:rows] + both_x[rows:])
        coded_g, scale_g = code(both_g[:rows] + both_g[rows:])
        scale_g = scale_g * factor_ref[...]
        for target in range(group):
            at = slice(target * own, (target + 1) * own)
            send[target, h] = jnp.concatenate([coded_x[at], coded_g[at]], axis=0).astype(jnp.int16)
            scales[target, 0:own] = jnp.where(lanes == h, scale_x[at], scales[target, 0:own])
            scales[target, own : 2 * own] = jnp.where(
                lanes == h, scale_g[at], scales[target, own : 2 * own]
            )
    for step in range(1, group):
        sums_copy(step_now, step, False).start()
    own_copy(step_now).start()

    @pl.when(step_now == chunks - 1)
    def _():
        for step in range(1, group):
            scales_copy(step, False).start()
        scale_own = pltpu.make_async_copy(scales.at[me], scales_ref.at[me], scale_own_sem)
        scale_own.start()

        def finish(chunk, carry):
            for step in range(1, group):
                sums_copy(chunk, step, False).wait_send()
                sums_copy(chunk, step, True).wait_recv()
            own_copy(chunk).wait()
            return carry

        lax.fori_loop(0, chunks, finish, 0)
        for step in range(1, group):
            scales_copy(step, False).wait_send()
            scales_copy(step, True).wait_recv()
        scale_own.wait()
        for step in range(1, lat_count):
            for copy in side_copies(step, False):
                copy.wait_send()
            for copy in side_copies(step, True):
                copy.wait_recv()
        for copy in side_own():
            copy.wait()


def code_rows(values):
    most = jnp.maximum(jnp.max(jnp.abs(values), axis=1, keepdims=True), LEAST)
    power = jnp.ceil(jnp.log(most) * (1.0 / math.log(2.0)) + 0.01)
    lanes = lax.broadcasted_iota(jnp.int32, values.shape, 1)
    coded = jnp.where(lanes == 127, power, jnp.round(values * jnp.exp2(15.0 - power)))
    return coded.astype(jnp.int32).astype(jnp.int16)


def decode_rows(coded):
    values = coded.astype(jnp.int32).astype(jnp.float32)
    return values * jnp.exp2(pick(values, 127) - 15.0)


def gelu_and_slope(values):
    root = math.sqrt(2.0 / math.pi)
    square = values * values
    tanh = jnp.tanh(root * (values + 0.044715 * (square * values)))
    half = 0.5 * (1.0 + tanh)
    slope = half + 0.5 * values * (1.0 - tanh * tanh) * (root * (1.0 + 3.0 * 0.044715 * square))
    return values * half, slope


def spectral_kernel(
    group, lat_count, sums_ref, scales_ref, there_high, there_low, back_high, back_low,
    first_ref, second_ref, bias_ref, mask_ref,
    coded_ref, coded_scales_ref, grads_ref,
    line, send, scales, whole, piece, pieces, pieces_in, sums, send_sem, recv_sem, own_sem,
    scale_send_sem, scale_recv_sem, scale_own_sem, piece_send_sem, piece_recv_sem,
    sum_send_sem, sum_recv_sem,
):
    me = place(lat_count)
    lon_count = group // lat_count
    lat_rows, mode_rows, chans = sums_ref.shape[1:]
    greet(group, lat_count)

    def gather(h, carry):
        for part in range(lat_count):
            total = None
            for lon in range(lon_count):
                source = lon * lat_count + part
                term = sums_ref[source, h].astype(jnp.int32).astype(jnp.float32) * pick(
                    scales_ref[source], h
                )
                total = term if total is None else total + term
            start = pl.multiple_of((part * lat_rows + h) * mode_rows, mode_rows)
            line[pl.ds(start, mode_rows), :] = total
        return carry

    lax.fori_loop(0, lat_rows, gather, 0)
    fields = dot_both((there_high[...], there_low[...]), split(line[...]))
    rows = fields.shape[0] // 4
    mask = mask_ref[...]
    spec = jnp.concatenate([fields[:rows], fields[rows : 2 * rows]], axis=1)
    out = jnp.concatenate(
        [fields[2 * rows : 3 * rows] * mask, fields[3 * rows :] * mask], axis=1
    )
    turned = ((1,), (1,))
    pre = dot_exact_right(spec, first_ref[...]) + bias_ref[...]
    act, slope = gelu_and_slope(pre)
    pre_grad = dot_exact_right(out, second_ref[...], turned) * slope
    spec_grad = dot_exact_right(pre_grad, first_ref[...], turned)
    spec_grad = jnp.concatenate([spec_grad[:, :chans], spec_grad[:, chans:]], axis=0)
    back = dot_both((back_high[...], back_low[...]), split(spec_grad))
    coded, scale = code(back)
    pairs = send.shape[1]
    send[...] = coded.astype(jnp.int16).reshape(send.shape)
    lanes = lax.broadcasted_iota(jnp.int32, (16, 128), 1)
    for part in range(lat_count):
        packed = jnp.zeros((16, 128), jnp.float32)
        for pair in range(pairs):
            start = (part * pairs + pair) * 16
            packed = jnp.where(lanes == pair, scale[start : start + 16], packed)
        scales[part] = packed

    def copies(step, arriving):
        target = lax.rem(me + step, group)
        part = lax.rem(target, lat_count)
        slot = lax.rem(me + group - step, group) if arriving else me
        return [
            pltpu.make_async_remote_copy(
                src_ref=source.at[part],
                dst_ref=landing.at[slot],
                send_sem=sent.at[step],
                recv_sem=arrived.at[step],
                device_id=device(target, lat_count),
                device_id_type=MESH,
            )
            for source, landing, sent, arrived in (
                (send, coded_ref, send_sem, recv_sem),
                (scales, coded_scales_ref, scale_send_sem, scale_recv_sem),
            )
        ]

    for step in range(1, group):
        for copy in copies(step, False):
            copy.start()
    my_part = lax.axis_index("lat")
    own = pltpu.make_async_copy(send.at[my_part], coded_ref.at[me], own_sem)
    own_scale = pltpu.make_async_copy(scales.at[my_part], coded_scales_ref.at[me], scale_own_sem)
    own.start()
    own_scale.start()

    def weight_grad(left, right):
        left = jnp.concatenate([left[:, :chans], left[:, chans:]], axis=0)
        right_real, right_imag = right[:, :chans], right[:, chans:]
        right = jnp.concatenate(
            [
                jnp.concatenate([right_real, right_imag], axis=1),
                jnp.concatenate([right_imag, -right_real], axis=1),
            ],
            axis=0,
        )
        return dot_both(split(left), split(right), ((0,), (0,)))

    size = (grads_ref.shape[1] - 16) // 2
    mine = chans // size // lat_count
    whole[0, :chans] = weight_grad(spec, pre_grad)
    whole[1, :chans] = weight_grad(act, out)
    for which, rows_in in enumerate((pre_grad, out)):
        total = jnp.sum(rows_in, axis=0, keepdims=True)
        first_row = lax.broadcasted_iota(jnp.int32, (8, 2 * chans), 0) == 0
        whole[which, chans : chans + 8] = jnp.where(first_row, total, 0.0)
    piece[...] = jnp.zeros_like(piece)
    for target in range(group):
        which, offset = divmod(target // lat_count, mine)
        at = (target % lat_count * mine + offset) * size
        for part in range(2):
            lanes_at = slice(part * chans + at, part * chans + at + size)
            piece[part * size : (part + 1) * size, 0:size] = whole[
                which, at : at + size, lanes_at
            ]
            start = 2 * size + 8 * part
            piece[start : start + 8, 0:size] = whole[which, chans : chans + 8, lanes_at]
        pieces[target] = code_rows(piece[...])

    def piece_copy(step):
        target = lax.rem(me + step, group)
        return pltpu.make_async_remote_copy(
            src_ref=pieces.at[target],
            dst_ref=pieces_in.at[step],
            send_sem=piece_send_sem.at[step],
            recv_sem=piece_recv_sem.at[step],
            device_id=device(target, lat_count),
            device_id_type=MESH,
        )

    my_lon = lax.axis_index("lon")

    def sum_copy(step, arriving):
        slot = lax.rem(my_lon + lon_count - step, lon_count) if arriving else my_lon
        return pltpu.make_async_remote_copy(
            src_ref=sums.at[my_lon],
            dst_ref=sums.at[slot],
            send_sem=sum_send_sem.at[step],
            recv_sem=sum_recv_sem.at[step],
            device_id={"lon": lax.rem(my_lon + step, lon_count)},
            device_id_type=MESH,
        )

    for step in range(1, group):
        piece_copy(step).start()
    total = decode_rows(pieces[me])
    for step in range(1, group):
        piece_copy(step).wait_recv()
        total = total + decode_rows(pieces_in[step])
    lanes = lax.broadcasted_iota(jnp.int32, total.shape, 1)
    sums[my_lon] = code_rows(jnp.where(lanes < size, total, 0.0))
    for step in range(1, lon_count):
        sum_copy(step, False).start()
    for step in range(1, group):
        piece_copy(step).wait_send()
    for step in range(1, lon_count):
        sum_copy(step, False).wait_send()
        sum_copy(step, True).wait_recv()
    for lon in range(lon_count):
        grads_ref[lon] = decode_rows(sums[lon])
    for step in range(1, group):
        for copy in copies(step, False):
            copy.wait_send()
        for copy in copies(step, True):
            copy.wait_recv()
    own.wait()
    own_scale.wait()


def inverse_kernel(table_ref, coded_ref, scales_ref, out_ref):
    scale = pick(scales_ref[...], pl.program_id(0))
    values = coded_ref[:, 0].astype(jnp.int32).astype(jnp.float32) * scale
    group, rows, chans = values.shape
    for inside in range(2):
        part = values[:, inside * rows // 2 : (inside + 1) * rows // 2].reshape(
            group * rows // 2, chans
        )
        high, low = split(part)
        out_ref[inside] = dot(
            table_ref[...], jnp.concatenate([high, low, high], axis=0)
        ).astype(jnp.bfloat16)


def block_diagonal(weights):
    blocks, _, size, _ = weights.shape

    def spread(part):
        eye = jnp.eye(blocks, dtype=part.dtype)
        full = part[:, :, None, :] * eye[:, None, :, None]
        return full.reshape(blocks * size, blocks * size)

    real, imag = spread(weights[:, 0]), spread(weights[:, 1])
    return jnp.concatenate(
        [jnp.concatenate([real, imag], axis=1), jnp.concatenate([-imag, real], axis=1)], axis=0
    )


def on_device_coded(
    inputs, cotangent, first_weight, first_bias, second_weight, counts, keep_flags
):
    lat_rows, lon_cells, chans = inputs.shape
    lon_count, lat_count = lax.axis_size("lon"), lax.axis_size("lat")
    lon_place, lat_place = lax.axis_index("lon"), lax.axis_index("lat")
    group = lon_count * lat_count
    modes_lon = KM // lon_count
    modes_own = KM // group
    lat_total = lat_rows * lat_count
    mine = first_weight.shape[1]
    size = first_weight.shape[-1]
    blocks = mine * lat_count
    vmem = pl.BlockSpec(memory_space=pltpu.VMEM)
    hbm = pl.BlockSpec(memory_space=pl.ANY)

    lon_high, lon_low = np_split(lon_table(lon_cells * lon_count))
    table = np.concatenate([lon_high, lon_low], axis=0)
    table = table.reshape(4 * KM, lon_count, lon_cells).transpose(1, 0, 2)
    table = lax.dynamic_index_in_dim(jnp.asarray(table), lon_place, 0, keepdims=False)
    table_back = np.concatenate([lon_high, lon_high, lon_low], axis=0).T
    table_back = table_back.reshape(lon_count, lon_cells, 6 * KM)
    table_back = lax.dynamic_index_in_dim(jnp.asarray(table_back), lon_place, 0, keepdims=False)
    there, back = lat_tables(lat_total, modes_own)
    factor = np.full((2 * KM, 1), 2.0, np.float32)
    factor[:2] = 1.0

    own_modes = lon_place * modes_lon + jnp.arange(modes_lon, dtype=jnp.int32)
    cut = own_modes[:, None] < counts[0][None, :]
    mask = jnp.where(cut[None], keep_flags[:, :, 0, :].astype(jnp.float32), 0.0)
    small = jnp.concatenate([mask.reshape(-1), first_bias.reshape(-1)])
    used = small.size
    small = jnp.pad(small, (0, -used % 1024)).reshape(-1, 128)
    weights = jnp.stack([first_weight[0], second_weight[0]])
    per_chunk = 4
    chunks = lat_rows // per_chunk
    rows = 4 * modes_own
    dma = pltpu.SemaphoreType.DMA
    block = pl.BlockSpec((per_chunk, lon_cells, chans), lambda i: (i, 0, 0))
    sums, scales, weights, small = pl.pallas_call(
        functools.partial(forward_kernel, group, lat_count, chunks),
        grid=(chunks,),
        out_shape=(
            jax.ShapeDtypeStruct((group, lat_rows, rows, chans), jnp.int16),
            jax.ShapeDtypeStruct((group, rows, 128), jnp.float32),
            jax.ShapeDtypeStruct((lat_count, *weights.shape), weights.dtype),
            jax.ShapeDtypeStruct((lat_count, *small.shape), small.dtype),
        ),
        in_specs=[
            pl.BlockSpec(table.shape, lambda i: (0, 0)),
            pl.BlockSpec(factor.shape, lambda i: (0, 0)),
            hbm,
            hbm,
            block,
            block,
        ],
        out_specs=(hbm,) * 4,
        scratch_shapes=[
            pltpu.VMEM((group, lat_rows, rows, chans), jnp.int16),
            pltpu.VMEM((group, rows, 128), jnp.float32),
            dma((chunks, group)),
            dma((chunks, group)),
            dma((chunks,)),
            dma((group,)),
            dma((group,)),
            dma,
            dma((2, lat_count)),
            dma((2, lat_count)),
            dma((2,)),
        ],
        compiler_params=pltpu.CompilerParams(
            collective_id=0, has_side_effects=True, vmem_limit_bytes=40 * 2**20
        ),
        cost_estimate=pl.CostEstimate(
            flops=16 * KM * inputs.size, bytes_accessed=4 * inputs.size, transcendentals=0
        ),
    )(table, jnp.asarray(factor), weights, small, inputs, cotangent)

    small = small.reshape(lat_count, -1)[:, :used]
    mask = small[:, : mask.size].reshape(lat_count, lat_total, modes_lon, mine)
    mask = lax.dynamic_slice_in_dim(mask, lat_place * modes_own, modes_own, 2)
    mask = jnp.transpose(mask, (2, 1, 0, 3)).reshape(modes_own * lat_total, blocks)
    mask = jnp.repeat(mask, size, axis=1)
    bias = small[:, -first_bias.size :].reshape(blocks, 2, size)
    bias = jnp.transpose(bias, (1, 0, 2)).reshape(1, 2 * chans)
    first = block_diagonal(weights[:, 0].reshape(blocks, 2, size, size))
    second = block_diagonal(weights[:, 1].reshape(blocks, 2, size, size))

    pairs = lat_rows // 2
    piece = (2 * size + 16, 128)
    coded, coded_scales, grads = pl.pallas_call(
        functools.partial(spectral_kernel, group, lat_count),
        out_shape=(
            jax.ShapeDtypeStruct((group, pairs, 4 * modes_own, chans), jnp.int16),
            jax.ShapeDtypeStruct((group, 16, 128), jnp.float32),
            jax.ShapeDtypeStruct((lon_count, *piece), jnp.float32),
        ),
        in_specs=[vmem] * 10,
        out_specs=(hbm, hbm, vmem),
        scratch_shapes=[
            pltpu.VMEM((4 * modes_own * lat_total, chans), jnp.float32),
            pltpu.VMEM((lat_count, pairs, 4 * modes_own, chans), jnp.int16),
            pltpu.VMEM((lat_count, 16, 128), jnp.float32),
            pltpu.VMEM((2, chans + 8, 2 * chans), jnp.float32),
            pltpu.VMEM(piece, jnp.float32),
            pltpu.VMEM((group, *piece), jnp.int16),
            pltpu.VMEM((group, *piece), jnp.int16),
            pltpu.VMEM((lon_count, *piece), jnp.int16),
            dma((group,)),
            dma((group,)),
            dma,
            dma((group,)),
            dma((group,)),
            dma,
            dma((group,)),
            dma((group,)),
            dma((lon_count,)),
            dma((lon_count,)),
        ],
        compiler_params=pltpu.CompilerParams(
            collective_id=1, has_side_effects=True, vmem_limit_bytes=56 * 2**20
        ),
    )(
        sums,
        scales,
        *(jnp.asarray(part) for part in np_split(there)),
        *(jnp.asarray(part) for part in np_split(back)),
        first,
        second,
        bias,
        mask,
    )

    weight_grads = grads[:, : 2 * size, :size].reshape(2, 1, mine, 2, size, size)
    bias_grads = grads[:, 2 * size :: 8, :size].reshape(2, 1, mine, 2, size)

    input_grad = pl.pallas_call(
        inverse_kernel,
        grid=(pairs,),
        out_shape=jax.ShapeDtypeStruct(inputs.shape, jnp.bfloat16),
        in_specs=[
            pl.BlockSpec(table_back.shape, lambda i: (0, 0)),
            pl.BlockSpec((group, 1, 4 * modes_own, chans), lambda i: (0, i, 0, 0)),
            pl.BlockSpec((group, 16, 128), lambda i: (0, 0, 0)),
        ],
        out_specs=pl.BlockSpec((2, lon_cells, chans), lambda i: (i, 0, 0)),
        compiler_params=pltpu.CompilerParams(vmem_limit_bytes=32 * 2**20),
        cost_estimate=pl.CostEstimate(
            flops=12 * KM * inputs.size, bytes_accessed=2 * inputs.size, transcendentals=0
        ),
    )(table_back, coded, coded_scales)
    return (
        input_grad,
        weight_grads[0],
        weight_grads[1],
        bias_grads[0],
        bias_grads[1],
    )


def solution(mesh):
    group = mesh.shape["lon"] * mesh.shape["lat"]
    body = on_device_coded if KM == 4 * group else on_device
    return jax.shard_map(
        body,
        mesh=mesh,
        in_specs=(
            P(("ens", "lat"), "lon", "ch"),
            P(("ens", "lat"), "lon", "ch"),
            P("ch", "lat", None, None, None),
            P("ch", "lat", None, None),
            P("ch", "lat", None, None, None),
            P("ch", "lat"),
            P(None, "lon", "ch", "lat"),
        ),
        out_specs=(
            P(("ens", "lat"), "lon", "ch"),
            P(("ens", "ch"), "lat", None, None, None),
            P(("ens", "ch"), "lat", None, None, None),
            P(("ens", "ch"), "lat", None, None),
            P(("ens", "ch"), "lat", None, None),
        ),
        check_vma=False,
    )
```

```python
import functools
import math

import jax
import jax.numpy as jnp
from jax import lax
from jax.experimental import pallas as pl
from jax.experimental.pallas import tpu as pltpu
from jax.sharding import PartitionSpec as P
import ml_dtypes
import numpy as np

KM = 32


exact_precision = lax.Precision.HIGHEST


def wave_tables(modes, cells, length):
    phase = (modes[:, None] * cells[None, :] % length).astype(jnp.float32)
    angle = phase * (2.0 * math.pi / length)
    scale = 1.0 / math.sqrt(length)
    return (jnp.cos(angle) * scale, jnp.sin(angle) * scale)


def activate(real_part, imag_part):
    return (jax.nn.gelu(real_part, approximate=True), jax.nn.gelu(imag_part, approximate=True))


def mixing_grads(spec_real, spec_imag, error_real, error_imag, weight_mask, first, bias, second):
    first_real = first[:, 0].astype(jnp.float32)
    first_imag = first[:, 1].astype(jnp.float32)
    second_real = second[:, 0].astype(jnp.float32)
    second_imag = second[:, 1].astype(jnp.float32)

    def forward_mul(values, matrix):
        return jnp.einsum("rbi,bio->rbo", values, matrix, precision=exact_precision)

    def back_mul(values, matrix):
        return jnp.einsum("rbo,bio->rbi", values, matrix, precision=exact_precision)

    def outer_sum(left, right):
        return jnp.einsum("rbi,rbo->bio", left, right, precision=exact_precision)

    pre_real = (
        forward_mul(spec_real, first_real) - forward_mul(spec_imag, first_imag) + bias[None, :, 0]
    )
    pre_imag = (
        forward_mul(spec_real, first_imag) + forward_mul(spec_imag, first_real) + bias[None, :, 1]
    )
    (act_real, act_imag), backward = jax.vjp(activate, pre_real, pre_imag)
    out_real = error_real * weight_mask[..., None]
    out_imag = error_imag * weight_mask[..., None]
    hid_real = back_mul(out_real, second_real) + back_mul(out_imag, second_imag)
    hid_imag = back_mul(out_imag, second_real) - back_mul(out_real, second_imag)
    grad_real, grad_imag = backward((hid_real, hid_imag))
    in_real = back_mul(grad_real, first_real) + back_mul(grad_imag, first_imag)
    in_imag = back_mul(grad_imag, first_real) - back_mul(grad_real, first_imag)
    second_grad = jnp.stack(
        [
            outer_sum(act_real, out_real) + outer_sum(act_imag, out_imag),
            outer_sum(act_real, out_imag) - outer_sum(act_imag, out_real),
        ],
        axis=1,
    )
    first_grad = jnp.stack(
        [
            outer_sum(spec_real, grad_real) + outer_sum(spec_imag, grad_imag),
            outer_sum(spec_real, grad_imag) - outer_sum(spec_imag, grad_real),
        ],
        axis=1,
    )
    first_bias_grad = jnp.stack([jnp.sum(grad_real, axis=0), jnp.sum(grad_imag, axis=0)], axis=1)
    second_bias_grad = jnp.stack([jnp.sum(out_real, axis=0), jnp.sum(out_imag, axis=0)], axis=1)
    return (in_real, in_imag, first_grad, second_grad, first_bias_grad, second_bias_grad)


def lat_forward(lat_cos, lat_sin, real_part, imag_part):
    out_real = jnp.einsum(
        "qh,khc->kqc", lat_cos, real_part, precision=exact_precision
    ) + jnp.einsum("qh,khc->kqc", lat_sin, imag_part, precision=exact_precision)
    out_imag = jnp.einsum(
        "qh,khc->kqc", lat_cos, imag_part, precision=exact_precision
    ) - jnp.einsum("qh,khc->kqc", lat_sin, real_part, precision=exact_precision)
    return (out_real, out_imag)


def lat_adjoint(lat_cos, lat_sin, real_part, imag_part):
    out_real = jnp.einsum(
        "qh,kqc->khc", lat_cos, real_part, precision=exact_precision
    ) - jnp.einsum("qh,kqc->khc", lat_sin, imag_part, precision=exact_precision)
    out_imag = jnp.einsum(
        "qh,kqc->khc", lat_sin, real_part, precision=exact_precision
    ) + jnp.einsum("qh,kqc->khc", lat_cos, imag_part, precision=exact_precision)
    return (out_real, out_imag)


def on_device(inputs, cotangent, first_weight, first_bias, second_weight, counts, keep_flags):
    lat_rows, lon_cells, chan_local = inputs.shape
    lon_count = lax.axis_size("lon")
    lat_count = lax.axis_size("lat")
    lon_place = lax.axis_index("lon")
    modes_dev = KM // lon_count
    lon_total = lon_cells * lon_count
    lat_total = lat_rows * lat_count
    own_cells = lon_place * lon_cells + jnp.arange(lon_cells, dtype=jnp.int32)
    own_modes = lon_place * modes_dev + jnp.arange(modes_dev, dtype=jnp.int32)
    field_x = inputs.astype(jnp.float32)
    field_g = cotangent.astype(jnp.float32)
    cosine, sine = wave_tables(
        jnp.arange(modes_dev * lax.axis_size("lon"), dtype=jnp.int32), own_cells, lon_total
    )
    x_real = jnp.einsum("hwc,kw->khc", field_x, cosine, precision=exact_precision)
    x_imag = -jnp.einsum("hwc,kw->khc", field_x, sine, precision=exact_precision)
    g_real = jnp.einsum("hwc,kw->khc", field_g, cosine, precision=exact_precision)
    g_imag = -jnp.einsum("hwc,kw->khc", field_g, sine, precision=exact_precision)
    spectra = lax.psum_scatter(
        jnp.stack([x_real, x_imag, g_real, g_imag], axis=1), "lon", scatter_dimension=0, tiled=True
    )
    factor = jnp.where(own_modes == 0, 1.0, 2.0).astype(jnp.float32)
    unity = jnp.ones_like(factor)
    spectra = spectra * jnp.stack([unity, unity, factor, factor], axis=1)[:, :, None, None]
    blocks = lax.all_to_all(spectra, "lat", split_axis=3, concat_axis=2, tiled=True)
    chan_block = blocks.shape[3]
    block_size = first_weight.shape[-1]
    local_blocks = chan_block // block_size
    lat_index = jnp.arange(lat_total, dtype=jnp.int32)
    lat_cos, lat_sin = wave_tables(lat_index, lat_index, lat_total)
    spec_real, spec_imag = lat_forward(lat_cos, lat_sin, blocks[:, 0], blocks[:, 1])
    error_real, error_imag = lat_forward(lat_cos, lat_sin, blocks[:, 2], blocks[:, 3])
    rows = modes_dev * lat_total
    cut = (own_modes[:, None] < counts[0][None, :]).astype(jnp.float32)
    flags = jnp.transpose(keep_flags[:, :, 0, :].astype(jnp.float32), (1, 0, 2))
    weight_mask = (cut[:, None, :] * flags).reshape(rows, local_blocks)

    def as_rows(values):
        return values.reshape(rows, local_blocks, block_size)

    results = mixing_grads(
        as_rows(spec_real),
        as_rows(spec_imag),
        as_rows(error_real),
        as_rows(error_imag),
        weight_mask,
        first_weight[0],
        first_bias[0],
        second_weight[0],
    )
    in_real, in_imag, first_grad, second_grad, first_bias_grad, second_bias_grad = results
    first_grad, second_grad, first_bias_grad, second_bias_grad = lax.psum(
        (first_grad, second_grad, first_bias_grad, second_bias_grad), "lon"
    )
    back_real, back_imag = lat_adjoint(
        lat_cos,
        lat_sin,
        in_real.reshape(modes_dev, lat_total, chan_block),
        in_imag.reshape(modes_dev, lat_total, chan_block),
    )
    back = lax.all_to_all(
        jnp.stack([back_real, back_imag], axis=1), "lat", split_axis=2, concat_axis=3, tiled=True
    )
    piece = lax.all_gather(back, "lon", axis=0, tiled=True)
    cosine, sine = wave_tables(jnp.arange(piece.shape[0], dtype=jnp.int32), own_cells, lon_total)
    total = jnp.einsum("khc,kw->hwc", piece[:, 0], cosine, precision=exact_precision)
    input_grad = (
        total - jnp.einsum("khc,kw->hwc", piece[:, 1], sine, precision=exact_precision)
    ).astype(jnp.bfloat16)
    return (
        input_grad,
        first_grad[None],
        second_grad[None],
        first_bias_grad[None],
        second_bias_grad[None],
    )


MESH = pl.DeviceIdType.MESH
TOP = 32767.0
LEAST = 1e-30


def np_split(table):
    high = table.astype(ml_dtypes.bfloat16)
    low = (table - high.astype(np.float64)).astype(ml_dtypes.bfloat16)
    return high, low


def split(values):
    high = values.astype(jnp.bfloat16)
    low = (values - high.astype(jnp.float32)).astype(jnp.bfloat16)
    return high, low


def np_waves(modes, cells, length):
    angle = (modes[:, None] * cells[None, :] % length) * (2.0 * np.pi / length)
    return np.cos(angle) / np.sqrt(length), np.sin(angle) / np.sqrt(length)


def lon_table(length):
    cosine, sine = np_waves(np.arange(KM), np.arange(length), length)
    return np.stack([cosine, -sine], axis=1).reshape(2 * KM, length)


def lat_tables(length, modes):
    index = np.arange(length)
    cosine, sine = np_waves(index, index, length)
    there = np.zeros((2, 2, modes, length, length, 2, modes, 2))
    back = np.zeros((length, modes, 2, 2, modes, length))
    for k in range(modes):
        for f in range(2):
            there[f, 0, k, :, :, f, k, 0] = cosine
            there[f, 0, k, :, :, f, k, 1] = sine
            there[f, 1, k, :, :, f, k, 1] = cosine
            there[f, 1, k, :, :, f, k, 0] = -sine
        back[:, k, 0, 0, k, :] = cosine.T
        back[:, k, 0, 1, k, :] = -sine.T
        back[:, k, 1, 0, k, :] = sine.T
        back[:, k, 1, 1, k, :] = cosine.T
    rows = 4 * modes * length
    return there.reshape(rows, rows), back.reshape(rows // 2, rows // 2)


def dot(left, right, dims=((1,), (0,))):
    return lax.dot_general(left, right, (dims, ((), ())), preferred_element_type=jnp.float32)


def dot_exact_right(left, right, dims=((1,), (0,))):
    high, low = split(left)
    return dot(high, right, dims) + dot(low, right, dims)


def dot_both(left, right, dims=((1,), (0,))):
    left_high, left_low = left
    right_high, right_low = right
    return (
        dot(left_high, right_high, dims)
        + dot(left_high, right_low, dims)
        + dot(left_low, right_high, dims)
    )


def code(values):
    most = jnp.maximum(jnp.max(jnp.abs(values), axis=1, keepdims=True), LEAST)
    return jnp.round(values * (TOP / most)).astype(jnp.int32), most * (1.0 / TOP)


def pick(scales, lane):
    lanes = lax.broadcasted_iota(jnp.int32, scales.shape, scales.ndim - 1)
    return jnp.sum(jnp.where(lanes == lane, scales, 0.0), axis=-1, keepdims=True)


def place(lat_count):
    return lax.axis_index("lon") * lat_count + lax.axis_index("lat")


def device(number, lat_count):
    return {"lon": lax.div(number, lat_count), "lat": lax.rem(number, lat_count)}


def greet(group, lat_count):
    me = place(lat_count)
    barrier = pltpu.get_barrier_semaphore()
    for step in range(1, group):
        pl.semaphore_signal(
            barrier,
            inc=1,
            device_id=device(lax.rem(me + step, group), lat_count),
            device_id_type=MESH,
        )
    pl.semaphore_wait(barrier, group - 1)


def forward_kernel(
    group, lat_count, chunks, table_ref, factor_ref, weights_ref, small_ref, x_ref, g_ref,
    sums_ref, scales_ref, all_weights_ref, all_small_ref,
    send, scales, send_sem, recv_sem, own_sem, scale_send_sem, scale_recv_sem, scale_own_sem,
    side_send_sem, side_recv_sem, side_own_sem,
):
    step_now = pl.program_id(0)
    me = place(lat_count)
    per_chunk = x_ref.shape[0]
    rows = table_ref.shape[0] // 2
    own = rows // group

    def sums_copy(chunk, step, arriving):
        target = lax.rem(me + step, group)
        slot = lax.rem(me + group - step, group) if arriving else me
        here = pl.ds(chunk * per_chunk, per_chunk)
        return pltpu.make_async_remote_copy(
            src_ref=send.at[target, here],
            dst_ref=sums_ref.at[slot, here],
            send_sem=send_sem.at[chunk, step],
            recv_sem=recv_sem.at[chunk, step],
            device_id=device(target, lat_count),
            device_id_type=MESH,
        )

    def own_copy(chunk):
        here = pl.ds(chunk * per_chunk, per_chunk)
        return pltpu.make_async_copy(send.at[me, here], sums_ref.at[me, here], own_sem.at[chunk])

    def scales_copy(step, arriving):
        target = lax.rem(me + step, group)
        slot = lax.rem(me + group - step, group) if arriving else me
        return pltpu.make_async_remote_copy(
            src_ref=scales.at[target],
            dst_ref=scales_ref.at[slot],
            send_sem=scale_send_sem.at[step],
            recv_sem=scale_recv_sem.at[step],
            device_id=device(target, lat_count),
            device_id_type=MESH,
        )

    sides = ((weights_ref, all_weights_ref), (small_ref, all_small_ref))
    my_part = lax.axis_index("lat")

    def side_copies(step, arriving):
        target = lax.rem(my_part + step, lat_count)
        slot = lax.rem(my_part + lat_count - step, lat_count) if arriving else my_part
        return [
            pltpu.make_async_remote_copy(
                src_ref=source,
                dst_ref=landing.at[slot],
                send_sem=side_send_sem.at[which, step],
                recv_sem=side_recv_sem.at[which, step],
                device_id={"lat": target},
                device_id_type=MESH,
            )
            for which, (source, landing) in enumerate(sides)
        ]

    def side_own():
        return [
            pltpu.make_async_copy(source, landing.at[my_part], side_own_sem.at[which])
            for which, (source, landing) in enumerate(sides)
        ]

    @pl.when(step_now == 0)
    def _():
        greet(group, lat_count)
        for step in range(1, lat_count):
            for copy in side_copies(step, False):
                copy.start()
        for copy in side_own():
            copy.start()
        scales[...] = jnp.zeros_like(scales)

    table = table_ref[...]
    lanes = lax.broadcasted_iota(jnp.int32, (own, 128), 1)
    for inside in range(per_chunk):
        h = step_now * per_chunk + inside
        both_x = dot(table, x_ref[inside])
        both_g = dot(table, g_ref[inside])
        coded_x, scale_x = code(both_x[:rows] + both_x[rows:])
        coded_g, scale_g = code(both_g[:rows] + both_g[rows:])
        scale_g = scale_g * factor_ref[...]
        for target in range(group):
            at = slice(target * own, (target + 1) * own)
            send[target, h] = jnp.concatenate([coded_x[at], coded_g[at]], axis=0).astype(jnp.int16)
            scales[target, 0:own] = jnp.where(lanes == h, scale_x[at], scales[target, 0:own])
            scales[target, own : 2 * own] = jnp.where(
                lanes == h, scale_g[at], scales[target, own : 2 * own]
            )
    for step in range(1, group):
        sums_copy(step_now, step, False).start()
    own_copy(step_now).start()

    @pl.when(step_now == chunks - 1)
    def _():
        for step in range(1, group):
            scales_copy(step, False).start()
        scale_own = pltpu.make_async_copy(scales.at[me], scales_ref.at[me], scale_own_sem)
        scale_own.start()

        def finish(chunk, carry):
            for step in range(1, group):
                sums_copy(chunk, step, False).wait_send()
                sums_copy(chunk, step, True).wait_recv()
            own_copy(chunk).wait()
            return carry

        lax.fori_loop(0, chunks, finish, 0)
        for step in range(1, group):
            scales_copy(step, False).wait_send()
            scales_copy(step, True).wait_recv()
        scale_own.wait()
        for step in range(1, lat_count):
            for copy in side_copies(step, False):
                copy.wait_send()
            for copy in side_copies(step, True):
                copy.wait_recv()
        for copy in side_own():
            copy.wait()


def code_rows(values):
    most = jnp.maximum(jnp.max(jnp.abs(values), axis=1, keepdims=True), LEAST)
    power = jnp.ceil(jnp.log(most) * (1.0 / math.log(2.0)) + 0.01)
    lanes = lax.broadcasted_iota(jnp.int32, values.shape, 1)
    coded = jnp.where(lanes == 127, power, jnp.round(values * jnp.exp2(15.0 - power)))
    return coded.astype(jnp.int32).astype(jnp.int16)


def decode_rows(coded):
    values = coded.astype(jnp.int32).astype(jnp.float32)
    return values * jnp.exp2(pick(values, 127) - 15.0)


def gelu_and_slope(values):
    root = math.sqrt(2.0 / math.pi)
    square = values * values
    tanh = jnp.tanh(root * (values + 0.044715 * (square * values)))
    half = 0.5 * (1.0 + tanh)
    slope = half + 0.5 * values * (1.0 - tanh * tanh) * (root * (1.0 + 3.0 * 0.044715 * square))
    return values * half, slope


def spectral_kernel(
    group, lat_count, sums_ref, scales_ref, there_high, there_low, back_high, back_low,
    first_ref, second_ref, bias_ref, mask_ref,
    coded_ref, coded_scales_ref, grads_ref,
    line, send, scales, whole, piece, pieces, pieces_in, sums, send_sem, recv_sem, own_sem,
    scale_send_sem, scale_recv_sem, scale_own_sem, piece_send_sem, piece_recv_sem,
    sum_send_sem, sum_recv_sem,
):
    me = place(lat_count)
    lon_count = group // lat_count
    lat_rows, mode_rows, chans = sums_ref.shape[1:]
    greet(group, lat_count)

    def gather(h, carry):
        for part in range(lat_count):
            total = None
            for lon in range(lon_count):
                source = lon * lat_count + part
                term = sums_ref[source, h].astype(jnp.int32).astype(jnp.float32) * pick(
                    scales_ref[source], h
                )
                total = term if total is None else total + term
            start = pl.multiple_of((part * lat_rows + h) * mode_rows, mode_rows)
            line[pl.ds(start, mode_rows), :] = total
        return carry

    lax.fori_loop(0, lat_rows, gather, 0)
    fields = dot_both((there_high[...], there_low[...]), split(line[...]))
    rows = fields.shape[0] // 4
    mask = mask_ref[...]
    spec = jnp.concatenate([fields[:rows], fields[rows : 2 * rows]], axis=1)
    out = jnp.concatenate(
        [fields[2 * rows : 3 * rows] * mask, fields[3 * rows :] * mask], axis=1
    )
    turned = ((1,), (1,))
    pre = dot_exact_right(spec, first_ref[...]) + bias_ref[...]
    act, slope = gelu_and_slope(pre)
    pre_grad = dot_exact_right(out, second_ref[...], turned) * slope
    spec_grad = dot_exact_right(pre_grad, first_ref[...], turned)
    spec_grad = jnp.concatenate([spec_grad[:, :chans], spec_grad[:, chans:]], axis=0)
    back = dot_both((back_high[...], back_low[...]), split(spec_grad))
    coded, scale = code(back)
    pairs = send.shape[1]
    send[...] = coded.astype(jnp.int16).reshape(send.shape)
    lanes = lax.broadcasted_iota(jnp.int32, (16, 128), 1)
    for part in range(lat_count):
        packed = jnp.zeros((16, 128), jnp.float32)
        for pair in range(pairs):
            start = (part * pairs + pair) * 16
            packed = jnp.where(lanes == pair, scale[start : start + 16], packed)
        scales[part] = packed

    def copies(step, arriving):
        target = lax.rem(me + step, group)
        part = lax.rem(target, lat_count)
        slot = lax.rem(me + group - step, group) if arriving else me
        return [
            pltpu.make_async_remote_copy(
                src_ref=source.at[part],
                dst_ref=landing.at[slot],
                send_sem=sent.at[step],
                recv_sem=arrived.at[step],
                device_id=device(target, lat_count),
                device_id_type=MESH,
            )
            for source, landing, sent, arrived in (
                (send, coded_ref, send_sem, recv_sem),
                (scales, coded_scales_ref, scale_send_sem, scale_recv_sem),
            )
        ]

    def weight_grad(left, right):
        left = jnp.concatenate([left[:, :chans], left[:, chans:]], axis=0)
        right_real, right_imag = right[:, :chans], right[:, chans:]
        right = jnp.concatenate(
            [
                jnp.concatenate([right_real, right_imag], axis=1),
                jnp.concatenate([right_imag, -right_real], axis=1),
            ],
            axis=0,
        )
        return dot_both(split(left), split(right), ((0,), (0,)))

    size = (grads_ref.shape[1] - 16) // 2
    mine = chans // size // lat_count
    whole[0, :chans] = weight_grad(spec, pre_grad)
    whole[1, :chans] = weight_grad(act, out)
    for which, rows_in in enumerate((pre_grad, out)):
        total = jnp.sum(rows_in, axis=0, keepdims=True)
        first_row = lax.broadcasted_iota(jnp.int32, (8, 2 * chans), 0) == 0
        whole[which, chans : chans + 8] = jnp.where(first_row, total, 0.0)
    piece[...] = jnp.zeros_like(piece)
    for target in range(group):
        which, offset = divmod(target // lat_count, mine)
        at = (target % lat_count * mine + offset) * size
        for part in range(2):
            lanes_at = slice(part * chans + at, part * chans + at + size)
            piece[part * size : (part + 1) * size, 0:size] = whole[
                which, at : at + size, lanes_at
            ]
            start = 2 * size + 8 * part
            piece[start : start + 8, 0:size] = whole[which, chans : chans + 8, lanes_at]
        pieces[target] = code_rows(piece[...])

    def piece_copy(step):
        target = lax.rem(me + step, group)
        return pltpu.make_async_remote_copy(
            src_ref=pieces.at[target],
            dst_ref=pieces_in.at[step],
            send_sem=piece_send_sem.at[step],
            recv_sem=piece_recv_sem.at[step],
            device_id=device(target, lat_count),
            device_id_type=MESH,
        )

    my_lon = lax.axis_index("lon")

    def sum_copy(step, arriving):
        slot = lax.rem(my_lon + lon_count - step, lon_count) if arriving else my_lon
        return pltpu.make_async_remote_copy(
            src_ref=sums.at[my_lon],
            dst_ref=sums.at[slot],
            send_sem=sum_send_sem.at[step],
            recv_sem=sum_recv_sem.at[step],
            device_id={"lon": lax.rem(my_lon + step, lon_count)},
            device_id_type=MESH,
        )

    for step in range(1, group):
        piece_copy(step).start()
    for step in range(1, group):
        for copy in copies(step, False):
            copy.start()
    my_part = lax.axis_index("lat")
    own = pltpu.make_async_copy(send.at[my_part], coded_ref.at[me], own_sem)
    own_scale = pltpu.make_async_copy(scales.at[my_part], coded_scales_ref.at[me], scale_own_sem)
    own.start()
    own_scale.start()
    total = decode_rows(pieces[me])
    for step in range(1, group):
        piece_copy(step).wait_recv()
        total = total + decode_rows(pieces_in[step])
    lanes = lax.broadcasted_iota(jnp.int32, total.shape, 1)
    sums[my_lon] = code_rows(jnp.where(lanes < size, total, 0.0))
    for step in range(1, lon_count):
        sum_copy(step, False).start()
    for step in range(1, group):
        piece_copy(step).wait_send()
    for step in range(1, lon_count):
        sum_copy(step, False).wait_send()
        sum_copy(step, True).wait_recv()
    for lon in range(lon_count):
        grads_ref[lon] = decode_rows(sums[lon])
    for step in range(1, group):
        for copy in copies(step, False):
            copy.wait_send()
        for copy in copies(step, True):
            copy.wait_recv()
    own.wait()
    own_scale.wait()


def inverse_kernel(table_ref, coded_ref, scales_ref, out_ref):
    scale = pick(scales_ref[...], pl.program_id(0))
    values = coded_ref[:, 0].astype(jnp.int32).astype(jnp.float32) * scale
    group, rows, chans = values.shape
    for inside in range(2):
        part = values[:, inside * rows // 2 : (inside + 1) * rows // 2].reshape(
            group * rows // 2, chans
        )
        high, low = split(part)
        out_ref[inside] = dot(
            table_ref[...], jnp.concatenate([high, low, high], axis=0)
        ).astype(jnp.bfloat16)


def block_diagonal(weights):
    blocks, _, size, _ = weights.shape

    def spread(part):
        eye = jnp.eye(blocks, dtype=part.dtype)
        full = part[:, :, None, :] * eye[:, None, :, None]
        return full.reshape(blocks * size, blocks * size)

    real, imag = spread(weights[:, 0]), spread(weights[:, 1])
    return jnp.concatenate(
        [jnp.concatenate([real, imag], axis=1), jnp.concatenate([-imag, real], axis=1)], axis=0
    )


def on_device_coded(
    inputs, cotangent, first_weight, first_bias, second_weight, counts, keep_flags
):
    lat_rows, lon_cells, chans = inputs.shape
    lon_count, lat_count = lax.axis_size("lon"), lax.axis_size("lat")
    lon_place, lat_place = lax.axis_index("lon"), lax.axis_index("lat")
    group = lon_count * lat_count
    modes_lon = KM // lon_count
    modes_own = KM // group
    lat_total = lat_rows * lat_count
    mine = first_weight.shape[1]
    size = first_weight.shape[-1]
    blocks = mine * lat_count
    vmem = pl.BlockSpec(memory_space=pltpu.VMEM)
    hbm = pl.BlockSpec(memory_space=pl.ANY)

    lon_high, lon_low = np_split(lon_table(lon_cells * lon_count))
    table = np.concatenate([lon_high, lon_low], axis=0)
    table = table.reshape(4 * KM, lon_count, lon_cells).transpose(1, 0, 2)
    table = lax.dynamic_index_in_dim(jnp.asarray(table), lon_place, 0, keepdims=False)
    table_back = np.concatenate([lon_high, lon_high, lon_low], axis=0).T
    table_back = table_back.reshape(lon_count, lon_cells, 6 * KM)
    table_back = lax.dynamic_index_in_dim(jnp.asarray(table_back), lon_place, 0, keepdims=False)
    there, back = lat_tables(lat_total, modes_own)
    factor = np.full((2 * KM, 1), 2.0, np.float32)
    factor[:2] = 1.0

    own_modes = lon_place * modes_lon + jnp.arange(modes_lon, dtype=jnp.int32)
    cut = own_modes[:, None] < counts[0][None, :]
    mask = jnp.where(cut[None], keep_flags[:, :, 0, :].astype(jnp.float32), 0.0)
    small = jnp.concatenate([mask.reshape(-1), first_bias.reshape(-1)])
    used = small.size
    small = jnp.pad(small, (0, -used % 1024)).reshape(-1, 128)
    weights = jnp.stack([first_weight[0], second_weight[0]])
    per_chunk = 4
    chunks = lat_rows // per_chunk
    rows = 4 * modes_own
    dma = pltpu.SemaphoreType.DMA
    block = pl.BlockSpec((per_chunk, lon_cells, chans), lambda i: (i, 0, 0))
    sums, scales, weights, small = pl.pallas_call(
        functools.partial(forward_kernel, group, lat_count, chunks),
        grid=(chunks,),
        out_shape=(
            jax.ShapeDtypeStruct((group, lat_rows, rows, chans), jnp.int16),
            jax.ShapeDtypeStruct((group, rows, 128), jnp.float32),
            jax.ShapeDtypeStruct((lat_count, *weights.shape), weights.dtype),
            jax.ShapeDtypeStruct((lat_count, *small.shape), small.dtype),
        ),
        in_specs=[
            pl.BlockSpec(table.shape, lambda i: (0, 0)),
            pl.BlockSpec(factor.shape, lambda i: (0, 0)),
            hbm,
            hbm,
            block,
            block,
        ],
        out_specs=(hbm,) * 4,
        scratch_shapes=[
            pltpu.VMEM((group, lat_rows, rows, chans), jnp.int16),
            pltpu.VMEM((group, rows, 128), jnp.float32),
            dma((chunks, group)),
            dma((chunks, group)),
            dma((chunks,)),
            dma((group,)),
            dma((group,)),
            dma,
            dma((2, lat_count)),
            dma((2, lat_count)),
            dma((2,)),
        ],
        compiler_params=pltpu.CompilerParams(
            collective_id=0, has_side_effects=True, vmem_limit_bytes=40 * 2**20
        ),
        cost_estimate=pl.CostEstimate(
            flops=16 * KM * inputs.size, bytes_accessed=4 * inputs.size, transcendentals=0
        ),
    )(table, jnp.asarray(factor), weights, small, inputs, cotangent)

    small = small.reshape(lat_count, -1)[:, :used]
    mask = small[:, : mask.size].reshape(lat_count, lat_total, modes_lon, mine)
    mask = lax.dynamic_slice_in_dim(mask, lat_place * modes_own, modes_own, 2)
    mask = jnp.transpose(mask, (2, 1, 0, 3)).reshape(modes_own * lat_total, blocks)
    mask = jnp.repeat(mask, size, axis=1)
    bias = small[:, -first_bias.size :].reshape(blocks, 2, size)
    bias = jnp.transpose(bias, (1, 0, 2)).reshape(1, 2 * chans)
    first = block_diagonal(weights[:, 0].reshape(blocks, 2, size, size))
    second = block_diagonal(weights[:, 1].reshape(blocks, 2, size, size))

    pairs = lat_rows // 2
    piece = (2 * size + 16, 128)
    coded, coded_scales, grads = pl.pallas_call(
        functools.partial(spectral_kernel, group, lat_count),
        out_shape=(
            jax.ShapeDtypeStruct((group, pairs, 4 * modes_own, chans), jnp.int16),
            jax.ShapeDtypeStruct((group, 16, 128), jnp.float32),
            jax.ShapeDtypeStruct((lon_count, *piece), jnp.float32),
        ),
        in_specs=[vmem] * 10,
        out_specs=(hbm, hbm, vmem),
        scratch_shapes=[
            pltpu.VMEM((4 * modes_own * lat_total, chans), jnp.float32),
            pltpu.VMEM((lat_count, pairs, 4 * modes_own, chans), jnp.int16),
            pltpu.VMEM((lat_count, 16, 128), jnp.float32),
            pltpu.VMEM((2, chans + 8, 2 * chans), jnp.float32),
            pltpu.VMEM(piece, jnp.float32),
            pltpu.VMEM((group, *piece), jnp.int16),
            pltpu.VMEM((group, *piece), jnp.int16),
            pltpu.VMEM((lon_count, *piece), jnp.int16),
            dma((group,)),
            dma((group,)),
            dma,
            dma((group,)),
            dma((group,)),
            dma,
            dma((group,)),
            dma((group,)),
            dma((lon_count,)),
            dma((lon_count,)),
        ],
        compiler_params=pltpu.CompilerParams(
            collective_id=1, has_side_effects=True, vmem_limit_bytes=56 * 2**20
        ),
    )(
        sums,
        scales,
        *(jnp.asarray(part) for part in np_split(there)),
        *(jnp.asarray(part) for part in np_split(back)),
        first,
        second,
        bias,
        mask,
    )

    weight_grads = grads[:, : 2 * size, :size].reshape(2, 1, mine, 2, size, size)
    bias_grads = grads[:, 2 * size :: 8, :size].reshape(2, 1, mine, 2, size)

    input_grad = pl.pallas_call(
        inverse_kernel,
        grid=(pairs,),
        out_shape=jax.ShapeDtypeStruct(inputs.shape, jnp.bfloat16),
        in_specs=[
            pl.BlockSpec(table_back.shape, lambda i: (0, 0)),
            pl.BlockSpec((group, 1, 4 * modes_own, chans), lambda i: (0, i, 0, 0)),
            pl.BlockSpec((group, 16, 128), lambda i: (0, 0, 0)),
        ],
        out_specs=pl.BlockSpec((2, lon_cells, chans), lambda i: (i, 0, 0)),
        compiler_params=pltpu.CompilerParams(vmem_limit_bytes=32 * 2**20),
        cost_estimate=pl.CostEstimate(
            flops=12 * KM * inputs.size, bytes_accessed=2 * inputs.size, transcendentals=0
        ),
    )(table_back, coded, coded_scales)
    return (
        input_grad,
        weight_grads[0],
        weight_grads[1],
        bias_grads[0],
        bias_grads[1],
    )


def solution(mesh):
    group = mesh.shape["lon"] * mesh.shape["lat"]
    body = on_device_coded if KM == 4 * group else on_device
    return jax.shard_map(
        body,
        mesh=mesh,
        in_specs=(
            P(("ens", "lat"), "lon", "ch"),
            P(("ens", "lat"), "lon", "ch"),
            P("ch", "lat", None, None, None),
            P("ch", "lat", None, None),
            P("ch", "lat", None, None, None),
            P("ch", "lat"),
            P(None, "lon", "ch", "lat"),
        ),
        out_specs=(
            P(("ens", "lat"), "lon", "ch"),
            P(("ens", "ch"), "lat", None, None, None),
            P(("ens", "ch"), "lat", None, None, None),
            P(("ens", "ch"), "lat", None, None),
            P(("ens", "ch"), "lat", None, None),
        ),
        check_vma=False,
    )
```
